512 devices in a mesh: outer: 16 (over x, z_hi, core), inner: 32 (over y, z_lo).
Axes of the slice: x: 4, y: 4, z: 16 (z_hi: 2, z_lo: 8; z = z_hi * 8 + z_lo), core: 2. Of those that a mesh axis runs over, the one named last changes fastest.
Arguments:
- queries: bfloat16 [65536, 1024], P(('outer', 'inner')), may hold values from -24 to 24
- keys: bfloat16 [65536, 128], P(('outer', 'inner')), may hold values from -4 to 4
- values: bfloat16 [65536, 128], P(('outer', 'inner')), may hold values from -6 to 6
- grad_out: bfloat16 [65536, 1024], P(('outer', 'inner')), may hold values from -24 to 24
- doc_ids: int32 [512], replicated, may hold values from 0 to 23, never falling along the last dimension, each value on 1 to 32 neighbouring positions
- block_order: int32 [512], replicated, may hold values from 0 to 511, as said below
Outputs:
- grad_queries: bfloat16 [65536, 1024], P(('outer', 'inner'))
- grad_keys: bfloat16 [65536, 128], P(('outer', 'inner'))
- grad_values: bfloat16 [65536, 128], P(('outer', 'inner'))
The draws below stay inside these ranges and needn't reach their ends.
Inputs may be any that keep to these rules, and one draw needn't show every extreme that they name: `doc_ids`: never falling along the sequence; each document spans 1 to 32 blocks and one spans exactly 32. Stored block s holds sequence block block_order[s]; the stored blocks of each aligned run of 32 (those of one index of outer) hold a permutation of the same run of sequence blocks.
All inputs are finite; a program needn't handle non-finite values.
Results may differ from the reference program's by a relative error of at most 0.022.
Values may be sent and summed in bfloat16 or wider, within the bound.
No kernel may reach another device: no remote copies, remote signals or barrier semaphores. Data moves between devices by JAX's collectives and lax.ppermute only.
A program may use at most 64 MiB of HBM per device.

```python
import math
import jax
import jax.numpy as jnp
import numpy as np
from jax import lax

BLOCK = 128
HD = 128
HEADS = 8
TOK_DEV = 128
TOKENS = 65536
NBLK = 512
GROUP_BLOCKS = 32
N_OUTER = 16
N_INNER = 32


def draw_keys(key, part):
    key = jax.random.fold_in(key, 1)
    return jnp.clip(jax.random.normal(key, (TOKENS, HD), jnp.float32), -4.0, 4.0).astype(jnp.bfloat16)


def draw_queries(key, part):
    key = jax.random.fold_in(key, 2)
    return jnp.clip(jax.random.normal(key, (TOKENS, HEADS * HD), jnp.float32), -4.0, 4.0).astype(jnp.bfloat16)


def draw_block_order(key, part):
    key = jax.random.fold_in(key, 3)
    group_count = NBLK // GROUP_BLOCKS
    ranks = jax.random.randint(key, (group_count, GROUP_BLOCKS), 0, 2 ** 20, dtype=jnp.int32)
    ranks = ranks * GROUP_BLOCKS + jnp.arange(GROUP_BLOCKS, dtype=jnp.int32)[None, :]
    local_order = jnp.argsort(ranks, axis=1).astype(jnp.int32)
    offsets = jnp.arange(group_count, dtype=jnp.int32)[:, None] * GROUP_BLOCKS
    return (local_order + offsets).reshape(NBLK).astype(jnp.int32)


def block_levels(rng, shape, split, low, high):
    gain, own = 1.0, jax.random.fold_in(rng, 6)
    for axis_at, blocks in split:
        steps = jnp.exp(jax.random.uniform(jax.random.fold_in(own, axis_at), (blocks,), jnp.float32, low / len(split), high / len(split)))
        gain = gain * jnp.repeat(steps, shape[axis_at] // blocks).reshape([-1 if axis == axis_at else 1 for axis in range(len(shape))])
    return gain


def length_profile(count, total, reach, skew):
    weights = [(1 << 20) // math.isqrt(grade ** skew) + 1 for grade in range(2, count + 1)]
    spare, counts = total - reach - (count - 1), [1] * (count - 1)
    while spare > 0:
        movable = [i for i in range(count - 1) if counts[i] < reach]
        mass, left = sum([weights[i] for i in movable]), spare
        for i in movable:
            addition = min(reach - counts[i], max(1, left * weights[i] // mass), spare)
            counts[i] = counts[i] + addition
            spare = spare - addition
    return np.array([reach] + counts)


def uneven(stream_key, amount, total, bound, skew):
    if amount == 2:
        one = jax.random.randint(stream_key, (), max(1, total - bound), min(bound, total - 1) + 1)
        return jnp.stack([one, total - one])
    sizes = jnp.asarray(length_profile(amount, total, bound, skew), jnp.int32)
    twos = (amount - 1) // 2
    donor, taker = sizes[1:1 + 2 * twos:2], sizes[2:2 + 2 * twos:2]
    slack = jnp.minimum(donor - 1, bound - taker)
    moved = jax.random.randint(jax.random.fold_in(stream_key, 1), (twos,), 0, 1 << 20) % (slack + 1)
    sizes = sizes.at[1:1 + 2 * twos:2].set(donor - moved).at[2:2 + 2 * twos:2].set(taker + moved)
    return sizes[jax.random.permutation(jax.random.fold_in(stream_key, 2), amount)]


def bell_draw(own_key, extent, width, reach, shards=(), kind=jnp.bfloat16):
    factor_of = block_levels(own_key, extent, shards, -0.22, 0.18) if shards else 1.0
    array = jax.random.normal(own_key, extent, jnp.float32) * width * factor_of
    return jnp.minimum(jnp.maximum(array, -reach), reach).astype(kind)


def setup_inputs(seed: int = 0) -> dict:
    arg_keys = jax.random.split(jax.random.key(seed), 7)
    return {
        "queries": draw_queries(jax.random.fold_in(arg_keys[6], 71), 0),
        "keys": draw_keys(jax.random.fold_in(arg_keys[6], 71), 0),
        "values": bell_draw(arg_keys[2], (TOKENS, HD), 1.0, 6.0, ((0, 512),)),
        "grad_out": bell_draw(arg_keys[3], (TOKENS, HEADS * HD), 4.0, 24.0, ((0, 512),)),
        "doc_ids": jnp.searchsorted(jnp.cumsum(uneven(arg_keys[4], NBLK * 3 // (2 * GROUP_BLOCKS), NBLK, GROUP_BLOCKS, 2)), jnp.arange(NBLK), side="right").astype(jnp.int32),
        "block_order": draw_block_order(jax.random.fold_in(arg_keys[6], 71), 0),
    }


NEG = -1.0e30


def visibility(window_docs, my_doc, own_block):
    count = window_docs.shape[0]
    blocks = jnp.arange(count, dtype=jnp.int32)
    matches = window_docs == my_doc
    query_offset = jnp.arange(BLOCK, dtype=jnp.int32)[:, None, None]
    key_offset = jnp.arange(BLOCK, dtype=jnp.int32)[None, None, :]
    earlier = (blocks < own_block)[None, :, None]
    diagonal = (blocks == own_block)[None, :, None] & (key_offset <= query_offset)
    allowed = matches[None, :, None] & (earlier | diagonal)
    return allowed.reshape(BLOCK, count * BLOCK)


def block_grads(query_block, grad_block, key_window, value_window, visible):
    scale = HD ** -0.5
    highest = lax.Precision.HIGHEST
    query_wide = query_block.astype(jnp.float32).reshape(BLOCK, HEADS, HD)
    grad_wide = grad_block.astype(jnp.float32).reshape(BLOCK, HEADS, HD)
    key_wide = key_window.astype(jnp.float32)
    value_wide = value_window.astype(jnp.float32)
    scores = jnp.einsum("bhd,kd->hbk", query_wide, key_wide, precision=highest) * scale
    scores = jnp.where(visible[None], scores, NEG)
    row_max = jnp.max(scores, axis=-1, keepdims=True)
    total = jnp.sum(jnp.where(visible[None], jnp.exp(scores - row_max), 0.0), axis=-1, keepdims=True)
    log_total = row_max + jnp.log(total)
    probs = jnp.where(visible[None], jnp.exp(scores - log_total), 0.0)
    probs_low = lax.optimization_barrier(probs.astype(jnp.bfloat16)).astype(jnp.float32)
    attended = jnp.einsum("hbk,kd->hbd", probs_low, value_wide, precision=highest)
    delta = jnp.sum(attended * jnp.transpose(grad_wide, (1, 0, 2)), axis=-1, keepdims=True)
    prob_grad = jnp.einsum("bhd,kd->hbk", grad_wide, value_wide, precision=highest)
    score_grad = probs * (prob_grad - delta)
    score_low = lax.optimization_barrier(score_grad.astype(jnp.bfloat16)).astype(jnp.float32)
    grad_query = jnp.einsum("hbk,kd->bhd", score_low, key_wide, precision=highest) * scale
    key_grad = jnp.einsum("hbk,bhd->kd", score_low, query_wide, precision=highest) * scale
    value_grad = jnp.einsum("hbk,bhd->kd", probs_low, grad_wide, precision=highest)
    return grad_query.reshape(BLOCK, HEADS * HD), key_grad, value_grad


def add_into(target, addend, start):
    current = lax.dynamic_slice_in_dim(target, start, addend.shape[0], 0)
    return lax.dynamic_update_slice_in_dim(target, current + addend, start, 0)


def reference(queries, keys, values, grad_out, doc_ids, block_order):
    block_count = TOKENS // BLOCK
    per_device = TOK_DEV // BLOCK
    group_blocks = N_INNER * per_device
    device_count = N_OUTER * N_INNER
    numbers = jnp.arange(block_count, dtype=jnp.int32)
    inverse = jnp.zeros((block_count,), jnp.int32).at[block_order].set(numbers)

    def to_sequence(stored):
        return stored.reshape(block_count, BLOCK, HD)[inverse].reshape(block_count * BLOCK, HD)

    padding = jnp.zeros((group_blocks * BLOCK, HD), jnp.bfloat16)
    keys_padded = jnp.concatenate([padding, to_sequence(keys)], axis=0)
    values_padded = jnp.concatenate([padding, to_sequence(values)], axis=0)
    docs_padded = jnp.concatenate([jnp.full((group_blocks,), -1, jnp.int32), doc_ids.astype(jnp.int32)])
    queries_split = queries.reshape(device_count, TOK_DEV, HEADS * HD)
    grads_split = grad_out.reshape(device_count, TOK_DEV, HEADS * HD)
    order_split = block_order.reshape(device_count, per_device)

    def device_step(carry, inputs):
        key_total, value_total = carry
        device, query_rows, grad_rows, device_order = inputs
        group = device // N_INNER
        window_start = (group * group_blocks).astype(jnp.int32)
        key_span = lax.dynamic_slice_in_dim(keys_padded, window_start * BLOCK, 2 * group_blocks * BLOCK, 0)
        value_span = lax.dynamic_slice_in_dim(values_padded, window_start * BLOCK, 2 * group_blocks * BLOCK, 0)
        docs_span = lax.dynamic_slice_in_dim(docs_padded, window_start, 2 * group_blocks, 0)
        partial_keys = jnp.zeros((2 * group_blocks * BLOCK, HD), jnp.float32)
        partial_values = jnp.zeros((2 * group_blocks * BLOCK, HD), jnp.float32)
        query_grads = []
        for slot_index in range(per_device):
            position = device_order[slot_index].astype(jnp.int32)
            first = (position - window_start + 1).astype(jnp.int32)
            key_window = lax.dynamic_slice_in_dim(key_span, first * BLOCK, group_blocks * BLOCK, 0)
            value_window = lax.dynamic_slice_in_dim(value_span, first * BLOCK, group_blocks * BLOCK, 0)
            window_docs = lax.dynamic_slice_in_dim(docs_span, first, group_blocks, 0)
            visible = visibility(window_docs, doc_ids[position], group_blocks - 1)
            rows_lo = slot_index * BLOCK
            grad_query, key_grad, value_grad = block_grads(
                query_rows[rows_lo:rows_lo + BLOCK], grad_rows[rows_lo:rows_lo + BLOCK],
                key_window, value_window, visible)
            partial_keys = add_into(partial_keys, key_grad, first * BLOCK)
            partial_values = add_into(partial_values, value_grad, first * BLOCK)
            query_grads.append(grad_query.astype(jnp.bfloat16))
        rounded_keys = lax.optimization_barrier(partial_keys.astype(jnp.bfloat16)).astype(jnp.float32)
        rounded_values = lax.optimization_barrier(partial_values.astype(jnp.bfloat16)).astype(jnp.float32)
        key_total = add_into(key_total, rounded_keys, window_start * BLOCK)
        value_total = add_into(value_total, rounded_values, window_start * BLOCK)
        return (key_total, value_total), jnp.concatenate(query_grads, axis=0)

    total_rows = (block_count + group_blocks) * BLOCK
    start_totals = (jnp.zeros((total_rows, HD), jnp.float32), jnp.zeros((total_rows, HD), jnp.float32))
    devices = jnp.arange(device_count, dtype=jnp.int32)
    (key_total, value_total), grad_queries = lax.scan(
        device_step, start_totals, (devices, queries_split, grads_split, order_split))

    def to_storage(ordered):
        trimmed = ordered[group_blocks * BLOCK:].reshape(block_count, BLOCK, HD)
        return trimmed[block_order].reshape(TOKENS, HD)

    grad_keys = to_storage(key_total).astype(jnp.bfloat16)
    grad_values = to_storage(value_total).astype(jnp.bfloat16)
    return grad_queries.reshape(TOKENS, HEADS * HD), grad_keys, grad_values
```

```python
import functools

import jax
import jax.numpy as jnp
from jax import lax
from jax.experimental import pallas as pl
from jax.experimental.pallas import tpu as pltpu
from jax.sharding import PartitionSpec as P

BLOCK = 128
HD = 128
HEADS = 8
ROWS = HEADS * BLOCK
GROUP = 32
NY = 4
NZ = 8
CHUNK = 256
NEG = -1e30
SCALE = HD**-0.5
SCALE2 = SCALE * 1.4426950408889634
VMEM_LIMIT = 40 * 1024 * 1024


def dot_nt(a, b):
    return lax.dot_general(a, b, (((1,), (1,)), ((), ())), preferred_element_type=jnp.float32)


def dot_nn(a, b):
    return lax.dot_general(a, b, (((1,), (0,)), ((), ())), preferred_element_type=jnp.float32)


def dot_tn(a, b):
    return lax.dot_general(a, b, (((0,), (0,)), ((), ())), preferred_element_type=jnp.float32)


def stack_heads(refs, target):
    for r, ref in enumerate(refs):
        for h in range(HEADS):
            target[r * ROWS + h * BLOCK : r * ROWS + (h + 1) * BLOCK, :] = ref[
                :, h * HD : (h + 1) * HD
            ]


def place(low, high, target):
    half = low.shape[0]
    target[0:half, :] = low[...]
    target[half : 2 * half, :] = high[...]


def pair_visible(ids, docs, order, prior, r, s):
    outer, inner = ids[0], ids[1]
    flip = ((s & 1) << 2) | (s & 2) | ((s >> 2) & 1)
    q_pos = order[outer * GROUP + (inner ^ (r * NZ))]
    if prior:
        k_pos = order[jnp.maximum(outer - 1, 0) * GROUP + (inner ^ flip)]
        return (outer > 0) & (docs[q_pos] == docs[k_pos])
    k_pos = order[outer * GROUP + (inner ^ flip)]
    return (docs[q_pos] == docs[k_pos]) & (k_pos < q_pos)


def diagonal_mask():
    k_at = lax.broadcasted_iota(jnp.int32, (BLOCK, CHUNK), 0)
    q_at = lax.broadcasted_iota(jnp.int32, (BLOCK, CHUNK), 1) % BLOCK
    return k_at <= q_at


def for_pairs(ids, docs, order, prior, pair):
    if not prior:
        pair(0, 0, True)

    @pl.loop(0 if prior else 1, NY * NZ)
    def _(step):
        r = step // NZ
        s = step % NZ

        @pl.when(pair_visible(ids, docs, order, prior, r, s))
        def _():
            pair(r, s, False)


def stats_kernel(prior, *refs):
    ids, docs, order = refs[:3]
    q_refs, g_refs = refs[3:7], refs[7:11]
    low, high = refs[11:13]
    rest = refs[13:]
    if prior:
        before, rest = rest[0], rest[1:]
    stats, qs, gs, kv = rest
    stack_heads(q_refs, qs)
    stack_heads(g_refs, gs)
    place(low, high, kv)
    if prior:
        stats[...] = before[...]
    else:
        stats[0:NY, :] = jnp.full((NY, ROWS), NEG, jnp.float32)
        stats[NY : 3 * NY, :] = jnp.zeros((2 * NY, ROWS), jnp.float32)

    def pair(r, s, diagonal):
        key = kv[pl.ds(s * 2 * BLOCK, BLOCK), :]
        value = kv[pl.ds(s * 2 * BLOCK + BLOCK, BLOCK), :]
        for c in range(ROWS // CHUNK):
            rows = pl.ds(r * ROWS + c * CHUNK, CHUNK)
            cols = pl.ds(c * CHUNK, CHUNK)
            scores = dot_nt(key, qs[rows, :]) * SCALE2
            dprob = dot_nt(value, gs[rows, :])
            if diagonal:
                scores = jnp.where(diagonal_mask(), scores, NEG)
            top = stats[pl.ds(r, 1), cols]
            new_top = jnp.maximum(top, jnp.max(scores, axis=0, keepdims=True))
            factor = jnp.exp2(top - new_top)
            weights = jnp.exp2(scores - new_top)
            stats[pl.ds(r, 1), cols] = new_top
            stats[pl.ds(NY + r, 1), cols] = stats[pl.ds(NY + r, 1), cols] * factor + jnp.sum(
                weights, axis=0, keepdims=True
            )
            stats[pl.ds(2 * NY + r, 1), cols] = stats[
                pl.ds(2 * NY + r, 1), cols
            ] * factor + jnp.sum(weights * dprob, axis=0, keepdims=True)

    for_pairs(ids, docs, order, prior, pair)


def grads_kernel(prior, *refs):
    ids, docs, order = refs[:3]
    q_refs, g_refs = refs[3:7], refs[7:11]
    low, high = refs[11:13]
    stat_refs = refs[13:17]
    rest = refs[17:]
    if prior:
        outs, scratch = rest[:5], rest[5:]
    else:
        dq_before, rest = rest[0], rest[1:]
        outs, scratch = rest[:8], rest[8:]
    out_high, out_mid, out_one, out_zero = outs[:4]
    qs, gs, kv, lse, delta, w_low, d_low, dkv = scratch[:8]
    dq = outs[4] if prior else scratch[8]
    stack_heads(q_refs, qs)
    stack_heads(g_refs, gs)
    place(low, high, kv)
    dkv[...] = jnp.zeros_like(dkv)
    if prior:
        dq[...] = jnp.zeros_like(dq)
    else:
        dq[...] = dq_before[...]
    for r in range(NY):
        tops = [stat_refs[k][(r ^ k) : (r ^ k) + 1, :] for k in range(NY)]
        top = functools.reduce(jnp.maximum, tops)
        total = jnp.zeros_like(top)
        product = jnp.zeros_like(top)
        for k in range(NY):
            factor = jnp.exp2(tops[k] - top)
            at = r ^ k
            total = total + stat_refs[k][NY + at : NY + at + 1, :] * factor
            product = product + stat_refs[k][2 * NY + at : 2 * NY + at + 1, :] * factor
        lse[r : r + 1, :] = top + jnp.log2(total)
        delta[r : r + 1, :] = product / total

    def pair(r, s, diagonal):
        key = kv[pl.ds(s * 2 * BLOCK, BLOCK), :]
        value = kv[pl.ds(s * 2 * BLOCK + BLOCK, BLOCK), :]
        for c in range(ROWS // CHUNK):
            rows = pl.ds(r * ROWS + c * CHUNK, CHUNK)
            cols = pl.ds(c * CHUNK, CHUNK)
            scores = dot_nt(key, qs[rows, :]) * SCALE2
            dprob = dot_nt(value, gs[rows, :])
            probs = jnp.exp2(scores - lse[pl.ds(r, 1), cols])
            if diagonal:
                probs = jnp.where(diagonal_mask(), probs, 0.0)
            w_low[:, cols] = probs.astype(jnp.bfloat16)
            d_low[:, cols] = (probs * (dprob - delta[pl.ds(r, 1), cols])).astype(jnp.bfloat16)
        rows = pl.ds(r * ROWS, ROWS)
        dkv[pl.ds(s * 2 * BLOCK, BLOCK), :] += dot_nn(d_low[...], qs[rows, :])
        dkv[pl.ds(s * 2 * BLOCK + BLOCK, BLOCK), :] += dot_nn(w_low[...], gs[rows, :])
        dq[pl.ds(r * HD, HD), :] += dot_tn(key, d_low[...])

    for_pairs(ids, docs, order, prior, pair)

    for slots, out in (((4, 8), out_high), ((2, 4), out_mid), ((1, 2), out_one), ((0, 1), out_zero)):
        for at, s in enumerate(range(*slots)):
            lo = s * 2 * BLOCK
            to = at * 2 * BLOCK
            out[to : to + BLOCK, :] = (dkv[lo : lo + BLOCK, :] * SCALE).astype(jnp.bfloat16)
            out[to + BLOCK : to + 2 * BLOCK, :] = dkv[lo + BLOCK : lo + 2 * BLOCK, :].astype(
                jnp.bfloat16
            )
    if not prior:
        for r in range(NY):
            for h in range(HEADS):
                part = dq[r * HD : (r + 1) * HD, h * BLOCK : (h + 1) * BLOCK] * SCALE
                outs[4 + r][:, h * HD : (h + 1) * HD] = part.astype(jnp.bfloat16).T


def smem():
    return pl.BlockSpec(memory_space=pltpu.SMEM)


def vmem():
    return pl.BlockSpec(memory_space=pltpu.VMEM)


def common_scratch():
    return [
        pltpu.VMEM((NY * ROWS, HD), jnp.bfloat16),
        pltpu.VMEM((NY * ROWS, HD), jnp.bfloat16),
        pltpu.VMEM((NZ * 2 * BLOCK, HD), jnp.bfloat16),
    ]


def cost(matmuls, pairs):
    return pl.CostEstimate(
        flops=matmuls * pairs * 2 * ROWS * BLOCK * HD,
        bytes_accessed=4 * 1024 * 1024,
        transcendentals=pairs * ROWS * BLOCK,
    )


def run_stats(prior, scalars, q_slots, g_slots, low, high, before=None):
    args = (*scalars, *q_slots, *g_slots, low, high)
    if prior:
        args = (*args, before)
    return pl.pallas_call(
        functools.partial(stats_kernel, prior),
        out_shape=jax.ShapeDtypeStruct((3 * NY, ROWS), jnp.float32),
        in_specs=[smem()] * 3 + [vmem()] * (len(args) - 3),
        out_specs=vmem(),
        scratch_shapes=common_scratch(),
        compiler_params=pltpu.CompilerParams(vmem_limit_bytes=VMEM_LIMIT),
        cost_estimate=cost(2, 16),
    )(*args)


def run_grads(prior, scalars, q_slots, g_slots, low, high, stats, dq_before=None):
    args = (*scalars, *q_slots, *g_slots, low, high, *stats)
    outs = [jax.ShapeDtypeStruct((n * 2 * BLOCK, HD), jnp.bfloat16) for n in (4, 2, 1, 1)]
    scratch = common_scratch() + [
        pltpu.VMEM((NY, ROWS), jnp.float32),
        pltpu.VMEM((NY, ROWS), jnp.float32),
        pltpu.VMEM((BLOCK, ROWS), jnp.bfloat16),
        pltpu.VMEM((BLOCK, ROWS), jnp.bfloat16),
        pltpu.VMEM((NZ * 2 * BLOCK, HD), jnp.float32),
    ]
    if prior:
        outs.append(jax.ShapeDtypeStruct((NY * HD, ROWS), jnp.float32))
    else:
        args = (*args, dq_before)
        outs += [jax.ShapeDtypeStruct((BLOCK, HEADS * HD), jnp.bfloat16)] * NY
        scratch.append(pltpu.VMEM((NY * HD, ROWS), jnp.float32))
    return pl.pallas_call(
        functools.partial(grads_kernel, prior),
        out_shape=outs,
        in_specs=[smem()] * 3 + [vmem()] * (len(args) - 3),
        out_specs=[vmem()] * len(outs),
        scratch_shapes=scratch,
        compiler_params=pltpu.CompilerParams(vmem_limit_bytes=VMEM_LIMIT),
        cost_estimate=cost(5, 16),
    )(*args)


def swap(array, flip):
    return lax.ppermute(array, "inner", [(i, i ^ flip) for i in range(GROUP)])


def across(array, by, flip):
    outer = lax.axis_size("outer")
    pairs = [
        (o * GROUP + i, (o + by) * GROUP + (i ^ flip))
        for o in range(outer)
        if 0 <= o + by < outer
        for i in range(GROUP)
    ]
    return lax.ppermute(array, ("outer", "inner"), pairs)


def add_low(*terms):
    total = terms[0].astype(jnp.float32)
    for term in terms[1:]:
        total = total + term.astype(jnp.float32)
    return total.astype(jnp.bfloat16)


def shards(queries, keys, values, grad_out, doc_ids, block_order):
    one = 2 * BLOCK
    ids = jnp.stack([lax.axis_index("outer"), lax.axis_index("inner")]).astype(jnp.int32)
    scalars = (ids, doc_ids, block_order)
    own = jnp.concatenate([keys, values], axis=0)

    before0 = across(own, 1, 0)
    before4 = across(own, 1, 4)
    own4 = swap(own, 4)
    q1, g1 = swap(queries, NZ), swap(grad_out, NZ)
    q3, g3 = swap(queries, 3 * NZ), swap(grad_out, 3 * NZ)
    own_pair = jnp.concatenate([own, own4], axis=0)
    own2 = swap(own_pair, 2)
    own_low = jnp.concatenate([own_pair, own2], axis=0)
    own_high = swap(own_low, 1)
    before_pair = jnp.concatenate([before0, before4], axis=0)
    before2 = swap(before_pair, 2)
    before_low = jnp.concatenate([before_pair, before2], axis=0)
    before_high = swap(before_low, 1)
    q2, g2 = swap(q1, 3 * NZ), swap(g3, NZ)
    q_slots = (queries, q1, q2, q3)
    g_slots = (grad_out, g1, g2, g3)

    stats = run_stats(False, scalars, q_slots, g_slots, own_low, own_high)
    stats = run_stats(True, scalars, q_slots, g_slots, before_low, before_high, stats)
    all_stats = (stats, swap(stats, NZ), swap(stats, 2 * NZ), swap(stats, 3 * NZ))

    b_high, b_mid, b_one, b_zero, dq_before = run_grads(
        True, scalars, q_slots, g_slots, before_low, before_high, all_stats
    )
    b1 = swap(b_high, 1)
    o_high, o_mid, o_one, o_zero, dq0, dq1, dq2, dq3 = run_grads(
        False, scalars, q_slots, g_slots, own_low, own_high, all_stats, dq_before
    )
    b2 = swap(add_low(b_mid, b1[2 * one :]), 2)
    o1 = swap(o_high, 1)
    back0 = across(add_low(b_zero, b1[:one], b2[:one]), -1, 0)
    back4 = across(add_low(b_one, b1[one : 2 * one], b2[one:]), -1, 4)
    o2 = swap(add_low(o_mid, o1[2 * one :]), 2)
    e2 = swap(dq2, 2 * NZ)
    e1 = swap(dq1, NZ)
    e3 = swap(dq3, 3 * NZ)
    o4 = swap(add_low(o_one, o1[one : 2 * one], o2[one:]), 4)
    grad_queries = add_low(dq0, e1, e2, e3)
    totals = add_low(o_zero, o1[:one], o2[:one], o4, back0, back4)
    return grad_queries, totals[:BLOCK], totals[BLOCK:]


def solution(mesh):
    rows = P(("outer", "inner"), None)
    return jax.shard_map(
        shards,
        mesh=mesh,
        in_specs=(rows, rows, rows, rows, P(), P()),
        out_specs=(rows, rows, rows),
        check_vma=False,
    )
```

```python
import functools

import jax
import jax.numpy as jnp
from jax import lax
from jax.experimental import pallas as pl
from jax.experimental.pallas import tpu as pltpu
from jax.sharding import PartitionSpec as P

BLOCK = 128
HD = 128
HEADS = 8
ROWS = HEADS * BLOCK
GROUP = 32
BLOCKS = 512
FIRST = 4
SECOND = 3
NY = 4
NZ = 8
CHUNK = 256
NEG = -1e30
SCALE = HD**-0.5
SCALE2 = SCALE * 1.4426950408889634
VMEM_LIMIT = 40 * 1024 * 1024


def dot_nt(a, b):
    return lax.dot_general(a, b, (((1,), (1,)), ((), ())), preferred_element_type=jnp.float32)


def dot_nn(a, b):
    return lax.dot_general(a, b, (((1,), (0,)), ((), ())), preferred_element_type=jnp.float32)


def dot_tn(a, b):
    return lax.dot_general(a, b, (((0,), (0,)), ((), ())), preferred_element_type=jnp.float32)


def stack_heads(refs, qs, gs):
    for r, ref in enumerate(refs):
        for h in range(HEADS):
            to = r * ROWS + h * BLOCK
            qs[to : to + BLOCK, :] = ref[0:BLOCK, h * HD : (h + 1) * HD]
            gs[to : to + BLOCK, :] = ref[BLOCK : 2 * BLOCK, h * HD : (h + 1) * HD]


def place(low, high, target):
    pair = 4 * BLOCK
    for half, ref in enumerate((low, high)):
        for quarter in range(2):
            for before in range(2):
                lo = (2 * quarter + before) * pair
                to = (4 * before + 2 * half + quarter) * pair
                target[to : to + pair, :] = ref[lo : lo + pair, :]


def pair_visible(meta, before, r, s):
    outer, inner = meta[2 * BLOCKS], meta[2 * BLOCKS + 1]
    tail = (s & 2) | ((s >> 2) & 1)
    q_pos = meta[BLOCKS + outer * GROUP + (inner ^ (r * NZ))]
    if before:
        flip = jnp.where((s & 1) == 0, FIRST, SECOND) ^ tail
        k_pos = meta[BLOCKS + jnp.maximum(outer - 1, 0) * GROUP + (inner ^ flip)]
        return (outer > 0) & (meta[q_pos] == meta[k_pos])
    flip = ((s & 1) << 2) | tail
    k_pos = meta[BLOCKS + outer * GROUP + (inner ^ flip)]
    return (meta[q_pos] == meta[k_pos]) & (k_pos < q_pos)


def diagonal_mask():
    k_at = lax.broadcasted_iota(jnp.int32, (BLOCK, CHUNK), 0)
    q_at = lax.broadcasted_iota(jnp.int32, (BLOCK, CHUNK), 1) % BLOCK
    return k_at <= q_at


def for_pairs(meta, pair):
    pair(0, 0, True)

    @pl.loop(1, NY * NZ)
    def _(step):
        r = step // NZ
        s = step % NZ

        @pl.when(pair_visible(meta, False, r, s))
        def _():
            pair(r, s, False)

    @pl.loop(0, NY * NZ)
    def _(step):
        r = step // NZ
        s = step % NZ

        @pl.when(pair_visible(meta, True, r, s))
        def _():
            pair(r, s + NZ, False)


def stats_kernel(meta, qg0, qg1, qg2, qg3, low, high, stats, qs, gs, kv):
    stack_heads((qg0, qg1, qg2, qg3), qs, gs)
    place(low, high, kv)
    stats[0:NY, :] = jnp.full((NY, ROWS), NEG, jnp.float32)
    stats[NY : 3 * NY, :] = jnp.zeros((2 * NY, ROWS), jnp.float32)

    def pair(r, s, diagonal):
        key = kv[pl.ds(s * 2 * BLOCK, BLOCK), :]
        value = kv[pl.ds(s * 2 * BLOCK + BLOCK, BLOCK), :]
        for c in range(ROWS // CHUNK):
            rows = pl.ds(r * ROWS + c * CHUNK, CHUNK)
            cols = pl.ds(c * CHUNK, CHUNK)
            scores = dot_nt(key, qs[rows, :]) * SCALE2
            dprob = dot_nt(value, gs[rows, :])
            if diagonal:
                scores = jnp.where(diagonal_mask(), scores, NEG)
            top = stats[pl.ds(r, 1), cols]
            new_top = jnp.maximum(top, jnp.max(scores, axis=0, keepdims=True))
            factor = jnp.exp2(top - new_top)
            weights = jnp.exp2(scores - new_top)
            stats[pl.ds(r, 1), cols] = new_top
            stats[pl.ds(NY + r, 1), cols] = stats[pl.ds(NY + r, 1), cols] * factor + jnp.sum(
                weights, axis=0, keepdims=True
            )
            stats[pl.ds(2 * NY + r, 1), cols] = stats[
                pl.ds(2 * NY + r, 1), cols
            ] * factor + jnp.sum(weights * dprob, axis=0, keepdims=True)

    for_pairs(meta, pair)


def grads_kernel(meta, qg0, qg1, qg2, qg3, low, high, st0, st1, st2, st3, *rest):
    out_high, out_mid, own_one, own_zero, before_one, before_zero = rest[:6]
    dq_outs = rest[6:10]
    qs, gs, kv, lse, delta, w_low, d_low, dkv, dq = rest[10:]
    stat_refs = (st0, st1, st2, st3)
    stack_heads((qg0, qg1, qg2, qg3), qs, gs)
    place(low, high, kv)
    dkv[...] = jnp.zeros_like(dkv)
    dq[...] = jnp.zeros_like(dq)
    for r in range(NY):
        tops = [stat_refs[k][(r ^ k) : (r ^ k) + 1, :] for k in range(NY)]
        top = functools.reduce(jnp.maximum, tops)
        total = jnp.zeros_like(top)
        product = jnp.zeros_like(top)
        for k in range(NY):
            factor = jnp.exp2(tops[k] - top)
            at = r ^ k
            total = total + stat_refs[k][NY + at : NY + at + 1, :] * factor
            product = product + stat_refs[k][2 * NY + at : 2 * NY + at + 1, :] * factor
        lse[r : r + 1, :] = top + jnp.log2(total)
        delta[r : r + 1, :] = product / total

    def pair(r, s, diagonal):
        key = kv[pl.ds(s * 2 * BLOCK, BLOCK), :]
        value = kv[pl.ds(s * 2 * BLOCK + BLOCK, BLOCK), :]
        for c in range(ROWS // CHUNK):
            rows = pl.ds(r * ROWS + c * CHUNK, CHUNK)
            cols = pl.ds(c * CHUNK, CHUNK)
            scores = dot_nt(key, qs[rows, :]) * SCALE2
            dprob = dot_nt(value, gs[rows, :])
            probs = jnp.exp2(scores - lse[pl.ds(r, 1), cols])
            if diagonal:
                probs = jnp.where(diagonal_mask(), probs, 0.0)
            w_low[:, cols] = probs.astype(jnp.bfloat16)
            d_low[:, cols] = (probs * (dprob - delta[pl.ds(r, 1), cols])).astype(jnp.bfloat16)
        rows = pl.ds(r * ROWS, ROWS)
        dkv[pl.ds(s * 2 * BLOCK, BLOCK), :] += dot_nn(d_low[...], qs[rows, :])
        dkv[pl.ds(s * 2 * BLOCK + BLOCK, BLOCK), :] += dot_nn(w_low[...], gs[rows, :])
        dq[pl.ds(r * HD, HD), :] += dot_tn(key, d_low[...])

    for_pairs(meta, pair)

    def write(slots, out, at):
        for s in slots:
            lo = s * 2 * BLOCK
            out[at : at + BLOCK, :] = (dkv[lo : lo + BLOCK, :] * SCALE).astype(jnp.bfloat16)
            out[at + BLOCK : at + 2 * BLOCK, :] = dkv[lo + BLOCK : lo + 2 * BLOCK, :].astype(
                jnp.bfloat16
            )
            at += 2 * BLOCK

    write((4, 5, NZ + 4, NZ + 5, 6, 7, NZ + 6, NZ + 7), out_high, 0)
    write((2, 3, NZ + 2, NZ + 3), out_mid, 0)
    write((1,), own_one, 0)
    write((0,), own_zero, 0)
    write((NZ + 1,), before_one, 0)
    write((NZ,), before_zero, 0)
    for r in range(NY):
        for h in range(HEADS):
            part = dq[r * HD : (r + 1) * HD, h * BLOCK : (h + 1) * BLOCK] * SCALE
            dq_outs[r][:, h * HD : (h + 1) * HD] = part.astype(jnp.bfloat16).T


def smem():
    return pl.BlockSpec(memory_space=pltpu.SMEM)


def vmem():
    return pl.BlockSpec(memory_space=pltpu.VMEM)


def common_scratch():
    return [
        pltpu.VMEM((NY * ROWS, HD), jnp.bfloat16),
        pltpu.VMEM((NY * ROWS, HD), jnp.bfloat16),
        pltpu.VMEM((2 * NZ * 2 * BLOCK, HD), jnp.bfloat16),
    ]


def cost(matmuls, pairs):
    return pl.CostEstimate(
        flops=matmuls * pairs * 2 * ROWS * BLOCK * HD,
        bytes_accessed=4 * 1024 * 1024,
        transcendentals=pairs * ROWS * BLOCK,
    )


def run_stats(*args):
    return pl.pallas_call(
        stats_kernel,
        out_shape=jax.ShapeDtypeStruct((3 * NY, ROWS), jnp.float32),
        in_specs=[smem()] + [vmem()] * (len(args) - 1),
        out_specs=vmem(),
        scratch_shapes=common_scratch(),
        compiler_params=pltpu.CompilerParams(vmem_limit_bytes=VMEM_LIMIT),
        cost_estimate=cost(2, 20),
    )(*args)


def run_grads(*args):
    outs = [jax.ShapeDtypeStruct((n * 2 * BLOCK, HD), jnp.bfloat16) for n in (8, 4, 1, 1, 1, 1)]
    outs += [jax.ShapeDtypeStruct((BLOCK, HEADS * HD), jnp.bfloat16)] * NY
    return pl.pallas_call(
        grads_kernel,
        out_shape=outs,
        in_specs=[smem()] + [vmem()] * (len(args) - 1),
        out_specs=[vmem()] * len(outs),
        scratch_shapes=common_scratch()
        + [
            pltpu.VMEM((NY, ROWS), jnp.float32),
            pltpu.VMEM((NY, ROWS), jnp.float32),
            pltpu.VMEM((BLOCK, ROWS), jnp.bfloat16),
            pltpu.VMEM((BLOCK, ROWS), jnp.bfloat16),
            pltpu.VMEM((2 * NZ * 2 * BLOCK, HD), jnp.float32),
            pltpu.VMEM((NY * HD, ROWS), jnp.float32),
        ],
        compiler_params=pltpu.CompilerParams(vmem_limit_bytes=VMEM_LIMIT),
        cost_estimate=cost(5, 20),
    )(*args)


def swap(array, flip):
    return lax.ppermute(array, "inner", [(i, i ^ flip) for i in range(GROUP)])


def across(array, by, flip):
    outer = lax.axis_size("outer")
    pairs = [
        (o * GROUP + i, (o + by) * GROUP + (i ^ flip))
        for o in range(outer)
        if 0 <= o + by < outer
        for i in range(GROUP)
    ]
    return lax.ppermute(array, ("outer", "inner"), pairs)


def add_low(*terms):
    total = terms[0].astype(jnp.float32)
    for term in terms[1:]:
        total = total + term.astype(jnp.float32)
    return total.astype(jnp.bfloat16)


def shards(queries, keys, values, grad_out, doc_ids, block_order):
    one = 2 * BLOCK
    ids = jnp.stack([lax.axis_index("outer"), lax.axis_index("inner")]).astype(jnp.int32)
    meta = jnp.concatenate([doc_ids, block_order, ids])
    own = jnp.concatenate([keys, values], axis=0)
    qg0 = jnp.concatenate([queries, grad_out], axis=0)

    before_a = across(own, 1, FIRST)
    before_b = across(own, 1, SECOND)
    own4 = swap(own, 4)
    qg2 = swap(qg0, 2 * NZ)
    qg1 = swap(qg0, NZ)
    qg3 = swap(qg0, 3 * NZ)
    quad = jnp.concatenate([own, own4, before_a, before_b], axis=0)
    low = jnp.concatenate([quad, swap(quad, 2)], axis=0)
    high = swap(low, 1)
    inputs = (meta, qg0, qg1, qg2, qg3, low, high)

    stats = run_stats(*inputs)
    all_stats = (stats, swap(stats, NZ), swap(stats, 2 * NZ), swap(stats, 3 * NZ))
    d_high, d_mid, own_one, own_zero, before_one, before_zero, dq0, dq1, dq2, dq3 = run_grads(
        *inputs, *all_stats
    )

    near = swap(d_high, 1)
    e2 = swap(dq2, 2 * NZ)
    e1 = swap(dq1, NZ)
    e3 = swap(dq3, 3 * NZ)
    far = swap(add_low(d_mid, near[4 * one :]), 2)
    back_a = across(add_low(before_zero, near[2 * one : 3 * one], far[2 * one : 3 * one]), -1, FIRST)
    back_b = across(add_low(before_one, near[3 * one : 4 * one], far[3 * one :]), -1, SECOND)
    own_far = swap(add_low(own_one, near[one : 2 * one], far[one : 2 * one]), 4)
    grad_queries = add_low(dq0, e1, e2, e3)
    totals = add_low(own_zero, near[:one], far[:one], own_far, back_a, back_b)
    return grad_queries, totals[:BLOCK], totals[BLOCK:]


def solution(mesh):
    rows = P(("outer", "inner"), None)
    return jax.shard_map(
        shards,
        mesh=mesh,
        in_specs=(rows, rows, rows, rows, P(), P()),
        out_specs=(rows, rows, rows),
        check_vma=False,
    )
```

```python
import functools

import jax
import jax.numpy as jnp
from jax import lax
from jax.experimental import pallas as pl
from jax.experimental.pallas import tpu as pltpu
from jax.sharding import PartitionSpec as P

BLOCK = 128
HD = 128
HEADS = 8
ROWS = HEADS * BLOCK
GROUP = 32
BLOCKS = 512
FAR = 4
STATS = 16
LIST = 32
NY = 4
NZ = 8
CHUNK = 256
NEG = -1e30
SCALE = HD**-0.5
SCALE2 = SCALE * 1.4426950408889634
VMEM_LIMIT = 40 * 1024 * 1024


def dot_nt(a, b):
    return lax.dot_general(a, b, (((1,), (1,)), ((), ())), preferred_element_type=jnp.float32)


def dot_nn(a, b):
    return lax.dot_general(a, b, (((1,), (0,)), ((), ())), preferred_element_type=jnp.float32)


def dot_tn(a, b):
    return lax.dot_general(a, b, (((0,), (0,)), ((), ())), preferred_element_type=jnp.float32)


def stack_heads(refs, qs, gs):
    for r, ref in enumerate(refs):
        for h in range(HEADS):
            to = r * ROWS + h * BLOCK
            qs[to : to + BLOCK, :] = ref[0:BLOCK, h * HD : (h + 1) * HD]
            gs[to : to + BLOCK, :] = ref[BLOCK : 2 * BLOCK, h * HD : (h + 1) * HD]


def place(low, high, ks, vs):
    for half, ref in enumerate((low, high)):
        for at in range(8):
            quarter, before, odd = at // 4, (at // 2) % 2, at % 2
            lo = at * 2 * BLOCK
            to = (NZ * before + 4 * half + 2 * quarter + odd) * BLOCK
            ks[to : to + BLOCK, :] = ref[lo : lo + BLOCK, :]
            vs[to : to + BLOCK, :] = ref[lo + BLOCK : lo + 2 * BLOCK, :]


def list_pairs(meta, lists):
    outer, inner = meta[2 * BLOCKS], meta[2 * BLOCKS + 1]
    q_at = [meta[BLOCKS + outer * GROUP + (inner ^ (r * NZ))] for r in range(NY)]
    q_doc = [meta[at] for at in q_at]
    far = jnp.where(outer % 2 == 0, FAR, 0)
    k_at, k_doc = [], []
    for s in range(2 * NZ):
        flip = ((s & 1) << 2) | (s & 2) | ((s >> 2) & 1)
        if s < NZ:
            at = meta[BLOCKS + outer * GROUP + (inner ^ flip)]
            doc = meta[at]
        else:
            at = meta[BLOCKS + jnp.maximum(outer - 1, 0) * GROUP + (inner ^ flip ^ far)]
            doc = jnp.where(outer > 0, meta[at], -1)
        k_at.append(at)
        k_doc.append(doc)
    for r in range(NY):
        count = jnp.int32(0)
        for s in range(2 * NZ):
            if r == 0 and s == 0:
                continue
            sees = q_doc[r] == k_doc[s]
            if s < NZ:
                sees = sees & (k_at[s] < q_at[r])
            lists[r * LIST + count] = jnp.int32(s)
            count = count + sees.astype(jnp.int32)
        lists[r * LIST + count] = jnp.int32(0)
        lists[r * LIST + LIST - 1] = count


def diagonal_mask():
    k_at = lax.broadcasted_iota(jnp.int32, (BLOCK, CHUNK), 0)
    q_at = lax.broadcasted_iota(jnp.int32, (BLOCK, CHUNK), 1) % BLOCK
    return k_at <= q_at


def for_pairs(lists, pair):
    pair(0, (0,), 0.0, True)

    @pl.loop(0, NY)
    def _(r):
        count = lists[r * LIST + LIST - 1]

        @pl.loop(0, (count + 1) // 2)
        def _(j):
            at = r * LIST + 2 * j
            bias = jnp.where(2 * j + 1 < count, 0.0, -NEG)
            pair(r, (lists[at], lists[at + 1]), bias, False)


def rows_of(ref, slots):
    return jnp.concatenate([ref[pl.ds(s * BLOCK, BLOCK), :] for s in slots], axis=0)


def stats_kernel(meta, qg0, qg1, qg2, qg3, low, high, stats, qs, gs, ks, vs, lists):
    list_pairs(meta, lists)
    stack_heads((qg0, qg1, qg2, qg3), qs, gs)
    place(low, high, ks, vs)
    stats[0:NY, :] = jnp.full((NY, ROWS), NEG, jnp.float32)
    stats[NY:STATS, :] = jnp.zeros((STATS - NY, ROWS), jnp.float32)

    def pair(r, slots, bias, diagonal):
        key, value = rows_of(ks, slots), rows_of(vs, slots)
        for c in range(ROWS // CHUNK):
            rows = pl.ds(r * ROWS + c * CHUNK, CHUNK)
            cols = pl.ds(c * CHUNK, CHUNK)
            scores = dot_nt(key, qs[rows, :]) * SCALE2
            dprob = dot_nt(value, gs[rows, :])
            if diagonal:
                scores = jnp.where(diagonal_mask(), scores, NEG)
            biases = (0.0, bias)[: len(slots)]
            top = stats[pl.ds(r, 1), cols]
            new_top = top
            for i, less in enumerate(biases):
                part = scores[i * BLOCK : (i + 1) * BLOCK]
                new_top = jnp.maximum(new_top, jnp.max(part, axis=0, keepdims=True) - less)
            factor = jnp.exp2(top - new_top)
            total = stats[pl.ds(NY + r, 1), cols] * factor
            product = stats[pl.ds(2 * NY + r, 1), cols] * factor
            for i, less in enumerate(biases):
                half = slice(i * BLOCK, (i + 1) * BLOCK)
                weights = jnp.exp2(scores[half] - (new_top + less))
                total = total + jnp.sum(weights, axis=0, keepdims=True)
                product = product + jnp.sum(weights * dprob[half], axis=0, keepdims=True)
            stats[pl.ds(r, 1), cols] = new_top
            stats[pl.ds(NY + r, 1), cols] = total
            stats[pl.ds(2 * NY + r, 1), cols] = product

    for_pairs(lists, pair)


def grads_kernel(meta, lists, qs, gs, ks, vs, stats, *rest):
    out_high, out_mid, own_one, own_zero, before_one, before_zero = rest[:6]
    dq_outs = rest[6:10]
    lse, delta, w_low, d_low, dk, dv, dq = rest[10:]
    dk[...] = jnp.zeros_like(dk)
    dv[...] = jnp.zeros_like(dv)
    dq[...] = jnp.zeros_like(dq)
    me = meta[2 * BLOCKS + 1] // NZ
    for r in range(NY):
        tops, sums, products = [], [], []
        for y in range(NY):
            at = STATS * y + (y ^ me ^ r)
            tops.append(stats[pl.ds(at, 1), :])
            sums.append(stats[pl.ds(at + NY, 1), :])
            products.append(stats[pl.ds(at + 2 * NY, 1), :])
        top = functools.reduce(jnp.maximum, tops)
        factors = [jnp.exp2(t - top) for t in tops]
        total = sum(x * f for x, f in zip(sums, factors))
        product = sum(x * f for x, f in zip(products, factors))
        lse[r : r + 1, :] = top + jnp.log2(total)
        delta[r : r + 1, :] = product / total

    def pair(r, slots, bias, diagonal):
        key, value = rows_of(ks, slots), rows_of(vs, slots)
        count = len(slots) * BLOCK
        for c in range(ROWS // CHUNK):
            rows = pl.ds(r * ROWS + c * CHUNK, CHUNK)
            cols = pl.ds(c * CHUNK, CHUNK)
            scores = dot_nt(key, qs[rows, :]) * SCALE2
            dprob = dot_nt(value, gs[rows, :])
            for i, less in enumerate((0.0, bias)[: len(slots)]):
                half = slice(i * BLOCK, (i + 1) * BLOCK)
                probs = jnp.exp2(scores[half] - (lse[pl.ds(r, 1), cols] + less))
                if diagonal:
                    probs = jnp.where(diagonal_mask(), probs, 0.0)
                w_low[half, cols] = probs.astype(jnp.bfloat16)
                dscore = probs * (dprob[half] - delta[pl.ds(r, 1), cols])
                d_low[half, cols] = dscore.astype(jnp.bfloat16)
        rows = pl.ds(r * ROWS, ROWS)
        dk_part = dot_nn(d_low[0:count, :], qs[rows, :])
        dv_part = dot_nn(w_low[0:count, :], gs[rows, :])
        for i, s in enumerate(slots):
            half = slice(i * BLOCK, (i + 1) * BLOCK)
            dk[pl.ds(s * BLOCK, BLOCK), :] += dk_part[half]
            dv[pl.ds(s * BLOCK, BLOCK), :] += dv_part[half]
        dq[pl.ds(r * HD, HD), :] += dot_tn(key, d_low[0:count, :])

    for_pairs(lists, pair)

    def write(slots, out, at):
        for s in slots:
            rows = slice(s * BLOCK, (s + 1) * BLOCK)
            out[at : at + BLOCK, :] = (dk[rows, :] * SCALE).astype(jnp.bfloat16)
            out[at + BLOCK : at + 2 * BLOCK, :] = dv[rows, :].astype(jnp.bfloat16)
            at += 2 * BLOCK

    write((4, 5, NZ + 4, NZ + 5, 6, 7, NZ + 6, NZ + 7), out_high, 0)
    write((2, 3, NZ + 2, NZ + 3), out_mid, 0)
    write((1,), own_one, 0)
    write((0,), own_zero, 0)
    write((NZ + 1,), before_one, 0)
    write((NZ,), before_zero, 0)
    for r in range(NY):
        for h in range(HEADS):
            part = dq[r * HD : (r + 1) * HD, h * BLOCK : (h + 1) * BLOCK] * SCALE
            dq_outs[r][:, h * HD : (h + 1) * HD] = part.astype(jnp.bfloat16).T


def smem():
    return pl.BlockSpec(memory_space=pltpu.SMEM)


def vmem():
    return pl.BlockSpec(memory_space=pltpu.VMEM)


def cost(matmuls, pairs):
    return pl.CostEstimate(
        flops=matmuls * pairs * 2 * ROWS * BLOCK * HD,
        bytes_accessed=4 * 1024 * 1024,
        transcendentals=pairs * ROWS * BLOCK,
    )


def run_stats(*args):
    stacked = jax.ShapeDtypeStruct((NY * ROWS, HD), jnp.bfloat16)
    blocks = jax.ShapeDtypeStruct((2 * NZ * BLOCK, HD), jnp.bfloat16)
    return pl.pallas_call(
        stats_kernel,
        out_shape=[
            jax.ShapeDtypeStruct((STATS, ROWS), jnp.float32),
            stacked,
            stacked,
            blocks,
            blocks,
            jax.ShapeDtypeStruct((NY * LIST,), jnp.int32),
        ],
        in_specs=[smem()] + [vmem()] * (len(args) - 1),
        out_specs=[vmem()] * 5 + [smem()],
        compiler_params=pltpu.CompilerParams(vmem_limit_bytes=VMEM_LIMIT),
        cost_estimate=cost(2, 20),
    )(*args)


def run_grads(*args):
    outs = [jax.ShapeDtypeStruct((n * 2 * BLOCK, HD), jnp.bfloat16) for n in (8, 4, 1, 1, 1, 1)]
    outs += [jax.ShapeDtypeStruct((BLOCK, HEADS * HD), jnp.bfloat16)] * NY
    return pl.pallas_call(
        grads_kernel,
        out_shape=outs,
        in_specs=[smem()] * 2 + [vmem()] * (len(args) - 2),
        out_specs=[vmem()] * len(outs),
        scratch_shapes=[
            pltpu.VMEM((NY, ROWS), jnp.float32),
            pltpu.VMEM((NY, ROWS), jnp.float32),
            pltpu.VMEM((2 * BLOCK, ROWS), jnp.bfloat16),
            pltpu.VMEM((2 * BLOCK, ROWS), jnp.bfloat16),
            pltpu.VMEM((2 * NZ * BLOCK, HD), jnp.float32),
            pltpu.VMEM((2 * NZ * BLOCK, HD), jnp.float32),
            pltpu.VMEM((NY * HD, ROWS), jnp.float32),
        ],
        compiler_params=pltpu.CompilerParams(vmem_limit_bytes=VMEM_LIMIT),
        cost_estimate=cost(5, 20),
    )(*args)


def swap(array, flip):
    return lax.ppermute(array, "inner", [(i, i ^ flip) for i in range(GROUP)])


def across(array, by):
    outer = lax.axis_size("outer")
    pairs = [
        (o * GROUP + i, (o + by) * GROUP + (i ^ (0 if max(o, o + by) % 2 else FAR)))
        for o in range(outer)
        if 0 <= o + by < outer
        for i in range(GROUP)
    ]
    return lax.ppermute(array, ("outer", "inner"), pairs)


def add_low(*terms):
    total = terms[0].astype(jnp.float32)
    for term in terms[1:]:
        total = total + term.astype(jnp.float32)
    return total.astype(jnp.bfloat16)


def shards(queries, keys, values, grad_out, doc_ids, block_order):
    one = 2 * BLOCK
    ids = jnp.stack([lax.axis_index("outer"), lax.axis_index("inner")]).astype(jnp.int32)
    meta = jnp.concatenate([doc_ids, block_order, ids])
    own = jnp.concatenate([keys, values], axis=0)
    qg0 = jnp.concatenate([queries, grad_out], axis=0)

    own_pair = jnp.concatenate([own, swap(own, 4)], axis=0)
    before_pair = across(own_pair, 1)
    qg2 = swap(qg0, 2 * NZ)
    qg1 = swap(qg0, NZ)
    qg3 = swap(qg0, 3 * NZ)
    quad = jnp.concatenate([own_pair, before_pair], axis=0)
    quad, qg1, qg3 = lax.optimization_barrier((quad, qg1, qg3))
    low = jnp.concatenate([quad, swap(quad, 2)], axis=0)
    high = swap(low, 1)

    stats, qs, gs, ks, vs, lists = run_stats(meta, qg0, qg1, qg2, qg3, low, high)
    along_y = [[y * NZ + z for y in range(NY)] for z in range(NZ)]
    all_stats = lax.all_gather(stats, "inner", axis=0, tiled=True, axis_index_groups=along_y)
    d_high, d_mid, own_one, own_zero, before_one, before_zero, dq0, dq1, dq2, dq3 = run_grads(
        meta, lists, qs, gs, ks, vs, all_stats
    )

    near = swap(d_high, 1)
    e2 = swap(dq2, 2 * NZ)
    e1 = swap(dq1, NZ)
    e3 = swap(dq3, 3 * NZ)
    near, e1, e3 = lax.optimization_barrier((near, e1, e3))
    far = swap(add_low(d_mid, near[4 * one :]), 2)
    back = across(
        add_low(
            jnp.concatenate([before_zero, before_one], axis=0),
            near[2 * one : 4 * one],
            far[2 * one : 4 * one],
        ),
        -1,
    )
    own_far = swap(add_low(own_one, near[one : 2 * one], far[one : 2 * one], back[one:]), 4)
    grad_queries = add_low(dq0, e1, e2, e3)
    totals = add_low(own_zero, near[:one], far[:one], back[:one], own_far)
    return grad_queries, totals[:BLOCK], totals[BLOCK:]


def solution(mesh):
    rows = P(("outer", "inner"), None)
    return jax.shard_map(
        shards,
        mesh=mesh,
        in_specs=(rows, rows, rows, rows, P(), P()),
        out_specs=(rows, rows, rows),
        check_vma=False,
    )
```

```python
import functools

import jax
import jax.numpy as jnp
from jax import lax
from jax.experimental import pallas as pl
from jax.experimental.pallas import tpu as pltpu
from jax.sharding import PartitionSpec as P

BLOCK = 128
HD = 128
HEADS = 8
ROWS = HEADS * BLOCK
GROUP = 32
BLOCKS = 512
FAR = 4
STATS = 16
LIST = 16
NY = 4
NZ = 8
CHUNK = 256
NEG = -1e30
SCALE = HD**-0.5
SCALE2 = SCALE * 1.4426950408889634
VMEM_LIMIT = 40 * 1024 * 1024


def dot_nt(a, b):
    return lax.dot_general(a, b, (((1,), (1,)), ((), ())), preferred_element_type=jnp.float32)


def dot_nn(a, b):
    return lax.dot_general(a, b, (((1,), (0,)), ((), ())), preferred_element_type=jnp.float32)


def dot_tn(a, b):
    return lax.dot_general(a, b, (((0,), (0,)), ((), ())), preferred_element_type=jnp.float32)


def stack_heads(refs, qs, gs):
    for r, ref in enumerate(refs):
        for h in range(HEADS):
            to = r * ROWS + h * BLOCK
            qs[to : to + BLOCK, :] = ref[0:BLOCK, h * HD : (h + 1) * HD]
            gs[to : to + BLOCK, :] = ref[BLOCK : 2 * BLOCK, h * HD : (h + 1) * HD]


def place(low, high, ks, vs):
    for s in range(NZ):
        ref, lo, to = (low, high)[s // 4], (s % 4) * 2 * BLOCK, s * BLOCK
        ks[to : to + BLOCK, :] = ref[lo : lo + BLOCK, :]
        vs[to : to + BLOCK, :] = ref[lo + BLOCK : lo + 2 * BLOCK, :]


def list_pairs(meta, before, lists):
    outer, inner = meta[2 * BLOCKS], meta[2 * BLOCKS + 1]
    q_at = [meta[BLOCKS + outer * GROUP + (inner ^ (r * NZ))] for r in range(NY)]
    q_doc = [meta[at] for at in q_at]
    k_at, k_doc = [], []
    for s in range(NZ):
        flip = ((s & 1) << 2) | (s & 2) | ((s >> 2) & 1)
        if before:
            far = jnp.where(outer % 2 == 0, FAR, 0)
            at = meta[BLOCKS + jnp.maximum(outer - 1, 0) * GROUP + (inner ^ flip ^ far)]
            doc = jnp.where(outer > 0, meta[at], -1)
        else:
            at = meta[BLOCKS + outer * GROUP + (inner ^ flip)]
            doc = meta[at]
        k_at.append(at)
        k_doc.append(doc)
    for r in range(NY):
        count = jnp.int32(0)
        for s in range(NZ):
            if not before and r == 0 and s == 0:
                continue
            sees = q_doc[r] == k_doc[s]
            if not before:
                sees = sees & (k_at[s] < q_at[r])
            lists[r * LIST + count] = jnp.int32(s)
            count = count + sees.astype(jnp.int32)
        lists[r * LIST + count] = jnp.int32(0)
        lists[r * LIST + LIST - 1] = count


def diagonal_mask():
    k_at = lax.broadcasted_iota(jnp.int32, (BLOCK, CHUNK), 0)
    q_at = lax.broadcasted_iota(jnp.int32, (BLOCK, CHUNK), 1) % BLOCK
    return k_at <= q_at


def for_pairs(before, lists, pair):
    if not before:
        pair(0, (0,), 0.0, True)

    @pl.loop(0, NY)
    def _(r):
        count = lists[r * LIST + LIST - 1]

        @pl.loop(0, (count + 1) // 2)
        def _(j):
            at = r * LIST + 2 * j
            bias = jnp.where(2 * j + 1 < count, 0.0, -NEG)
            pair(r, (lists[at], lists[at + 1]), bias, False)


def rows_of(ref, slots):
    return jnp.concatenate([ref[pl.ds(s * BLOCK, BLOCK), :] for s in slots], axis=0)


def stats_kernel(before, *refs):
    if before:
        meta, low, high, qs, gs, earlier, stats, ks, vs, lists = refs
        stats[...] = earlier[...]
    else:
        meta, low, high, *qg, stats, ks, vs, lists, qs, gs = refs
        stack_heads(qg, qs, gs)
        stats[0:NY, :] = jnp.full((NY, ROWS), NEG, jnp.float32)
        stats[NY:STATS, :] = jnp.zeros((STATS - NY, ROWS), jnp.float32)
    list_pairs(meta, before, lists)
    place(low, high, ks, vs)

    def pair(r, slots, bias, diagonal):
        key, value = rows_of(ks, slots), rows_of(vs, slots)
        for c in range(ROWS // CHUNK):
            rows = pl.ds(r * ROWS + c * CHUNK, CHUNK)
            cols = pl.ds(c * CHUNK, CHUNK)
            scores = dot_nt(key, qs[rows, :]) * SCALE2
            dprob = dot_nt(value, gs[rows, :])
            if diagonal:
                scores = jnp.where(diagonal_mask(), scores, NEG)
            biases = (0.0, bias)[: len(slots)]
            top = stats[pl.ds(r, 1), cols]
            new_top = top
            for i, less in enumerate(biases):
                part = scores[i * BLOCK : (i + 1) * BLOCK]
                new_top = jnp.maximum(new_top, jnp.max(part, axis=0, keepdims=True) - less)
            factor = jnp.exp2(top - new_top)
            total = stats[pl.ds(NY + r, 1), cols] * factor
            product = stats[pl.ds(2 * NY + r, 1), cols] * factor
            for i, less in enumerate(biases):
                half = slice(i * BLOCK, (i + 1) * BLOCK)
                weights = jnp.exp2(scores[half] - (new_top + less))
                total = total + jnp.sum(weights, axis=0, keepdims=True)
                product = product + jnp.sum(weights * dprob[half], axis=0, keepdims=True)
            stats[pl.ds(r, 1), cols] = new_top
            stats[pl.ds(NY + r, 1), cols] = total
            stats[pl.ds(2 * NY + r, 1), cols] = product

    for_pairs(before, lists, pair)


def grads_kernel(meta, own_lists, before_lists, qs, gs, own_k, own_v, before_k, before_v, stats, *rest):
    b_high, b_mid, b_pair, o_high, o_mid, o_one, o_zero, dq0, dq12, dq3 = rest[:10]
    lse, delta, w_low, d_low, dk, dv, dq = rest[10:]
    dk[...] = jnp.zeros_like(dk)
    dv[...] = jnp.zeros_like(dv)
    dq[...] = jnp.zeros_like(dq)
    me = meta[2 * BLOCKS + 1] // NZ
    for r in range(NY):
        tops, sums, products = [], [], []
        for y in range(NY):
            at = STATS * y + (y ^ me ^ r)
            tops.append(stats[pl.ds(at, 1), :])
            sums.append(stats[pl.ds(at + NY, 1), :])
            products.append(stats[pl.ds(at + 2 * NY, 1), :])
        top = functools.reduce(jnp.maximum, tops)
        factors = [jnp.exp2(t - top) for t in tops]
        total = sum(x * f for x, f in zip(sums, factors))
        product = sum(x * f for x, f in zip(products, factors))
        lse[r : r + 1, :] = top + jnp.log2(total)
        delta[r : r + 1, :] = product / total

    def pair(ks, vs, base, r, slots, bias, diagonal):
        key, value = rows_of(ks, slots), rows_of(vs, slots)
        count = len(slots) * BLOCK
        for c in range(ROWS // CHUNK):
            rows = pl.ds(r * ROWS + c * CHUNK, CHUNK)
            cols = pl.ds(c * CHUNK, CHUNK)
            scores = dot_nt(key, qs[rows, :]) * SCALE2
            dprob = dot_nt(value, gs[rows, :])
            for i, less in enumerate((0.0, bias)[: len(slots)]):
                half = slice(i * BLOCK, (i + 1) * BLOCK)
                probs = jnp.exp2(scores[half] - (lse[pl.ds(r, 1), cols] + less))
                if diagonal:
                    probs = jnp.where(diagonal_mask(), probs, 0.0)
                w_low[half, cols] = probs.astype(jnp.bfloat16)
                dscore = probs * (dprob[half] - delta[pl.ds(r, 1), cols])
                d_low[half, cols] = dscore.astype(jnp.bfloat16)
        rows = pl.ds(r * ROWS, ROWS)
        dk_part = dot_nn(d_low[0:count, :], qs[rows, :])
        dv_part = dot_nn(w_low[0:count, :], gs[rows, :])
        for i, s in enumerate(slots):
            half = slice(i * BLOCK, (i + 1) * BLOCK)
            dk[pl.ds((base + s) * BLOCK, BLOCK), :] += dk_part[half]
            dv[pl.ds((base + s) * BLOCK, BLOCK), :] += dv_part[half]
        dq[pl.ds(r * HD, HD), :] += dot_tn(key, d_low[0:count, :])

    for_pairs(False, own_lists, functools.partial(pair, own_k, own_v, 0))
    for_pairs(True, before_lists, functools.partial(pair, before_k, before_v, NZ))

    def write(slots, out, at):
        for s in slots:
            rows = slice(s * BLOCK, (s + 1) * BLOCK)
            out[at : at + BLOCK, :] = (dk[rows, :] * SCALE).astype(jnp.bfloat16)
            out[at + BLOCK : at + 2 * BLOCK, :] = dv[rows, :].astype(jnp.bfloat16)
            at += 2 * BLOCK

    write((NZ + 4, NZ + 5, NZ + 6, NZ + 7), b_high, 0)
    write((NZ + 2, NZ + 3), b_mid, 0)
    write((NZ, NZ + 1), b_pair, 0)
    write((4, 5, 6, 7), o_high, 0)
    write((2, 3), o_mid, 0)
    write((1,), o_one, 0)
    write((0,), o_zero, 0)
    for r, (out, at) in enumerate(((dq0, 0), (dq12, 0), (dq12, BLOCK), (dq3, 0))):
        for h in range(HEADS):
            part = dq[r * HD : (r + 1) * HD, h * BLOCK : (h + 1) * BLOCK] * SCALE
            out[at : at + BLOCK, h * HD : (h + 1) * HD] = part.astype(jnp.bfloat16).T


def smem():
    return pl.BlockSpec(memory_space=pltpu.SMEM)


def vmem():
    return pl.BlockSpec(memory_space=pltpu.VMEM)


def cost(matmuls, pairs):
    return pl.CostEstimate(
        flops=matmuls * pairs * 2 * ROWS * BLOCK * HD,
        bytes_accessed=4 * 1024 * 1024,
        transcendentals=pairs * ROWS * BLOCK,
    )


def run_stats(before, *args):
    blocks = jax.ShapeDtypeStruct((NZ * BLOCK, HD), jnp.bfloat16)
    outs = [
        jax.ShapeDtypeStruct((STATS, ROWS), jnp.float32),
        blocks,
        blocks,
        jax.ShapeDtypeStruct((NY * LIST,), jnp.int32),
    ]
    specs = [vmem()] * 3 + [smem()]
    if not before:
        outs += [jax.ShapeDtypeStruct((NY * ROWS, HD), jnp.bfloat16)] * 2
        specs += [vmem()] * 2
    return pl.pallas_call(
        functools.partial(stats_kernel, before),
        out_shape=outs,
        in_specs=[smem()] + [vmem()] * (len(args) - 1),
        out_specs=specs,
        compiler_params=pltpu.CompilerParams(vmem_limit_bytes=VMEM_LIMIT),
        cost_estimate=cost(2, 10),
    )(*args)


def run_grads(*args):
    outs = [jax.ShapeDtypeStruct((n * 2 * BLOCK, HD), jnp.bfloat16) for n in (4, 2, 2, 4, 2, 1, 1)]
    outs += [jax.ShapeDtypeStruct((n * BLOCK, HEADS * HD), jnp.bfloat16) for n in (1, 2, 1)]
    return pl.pallas_call(
        grads_kernel,
        out_shape=outs,
        in_specs=[smem()] * 3 + [vmem()] * (len(args) - 3),
        out_specs=[vmem()] * len(outs),
        scratch_shapes=[
            pltpu.VMEM((NY, ROWS), jnp.float32),
            pltpu.VMEM((NY, ROWS), jnp.float32),
            pltpu.VMEM((2 * BLOCK, ROWS), jnp.bfloat16),
            pltpu.VMEM((2 * BLOCK, ROWS), jnp.bfloat16),
            pltpu.VMEM((2 * NZ * BLOCK, HD), jnp.float32),
            pltpu.VMEM((2 * NZ * BLOCK, HD), jnp.float32),
            pltpu.VMEM((NY * HD, ROWS), jnp.float32),
        ],
        compiler_params=pltpu.CompilerParams(vmem_limit_bytes=VMEM_LIMIT),
        cost_estimate=cost(5, 20),
    )(*args)


def swap(array, flip):
    return lax.ppermute(array, "inner", [(i, i ^ flip) for i in range(GROUP)])


def across(array, by):
    outer = lax.axis_size("outer")
    pairs = [
        (o * GROUP + i, (o + by) * GROUP + (i ^ (0 if max(o, o + by) % 2 else FAR)))
        for o in range(outer)
        if 0 <= o + by < outer
        for i in range(GROUP)
    ]
    return lax.ppermute(array, ("outer", "inner"), pairs)


def add_low(*terms):
    total = terms[0].astype(jnp.float32)
    for term in terms[1:]:
        total = total + term.astype(jnp.float32)
    return total.astype(jnp.bfloat16)


def shards(queries, keys, values, grad_out, doc_ids, block_order):
    one = 2 * BLOCK
    ids = jnp.stack([lax.axis_index("outer"), lax.axis_index("inner")]).astype(jnp.int32)
    meta = jnp.concatenate([doc_ids, block_order, ids])
    own = jnp.concatenate([keys, values], axis=0)
    qg0 = jnp.concatenate([queries, grad_out], axis=0)

    own4 = swap(own, 4)
    qg_later, _ = lax.optimization_barrier((qg0, own4))
    qg1 = swap(qg0, NZ)
    qg3 = swap(qg_later, 3 * NZ)
    qg2 = swap(qg_later, 2 * NZ)
    own_pair = jnp.concatenate([own, own4], axis=0)
    before_pair = across(own_pair, 1)
    own_low = jnp.concatenate([own_pair, swap(own_pair, 2)], axis=0)
    own_high = swap(own_low, 1)
    before_low = jnp.concatenate([before_pair, swap(before_pair, 2)], axis=0)
    before_low, qg1, qg2 = lax.optimization_barrier((before_low, qg1, qg2))
    before_high = swap(before_low, 1)

    stats, own_k, own_v, own_lists, qs, gs = run_stats(
        False, meta, own_low, own_high, qg0, qg1, qg2, qg3
    )
    stats, before_k, before_v, before_lists = run_stats(
        True, meta, before_low, before_high, qs, gs, stats
    )
    along_y = [[y * NZ + z for y in range(NY)] for z in range(NZ)]
    all_stats = lax.all_gather(stats, "inner", axis=0, tiled=True, axis_index_groups=along_y)
    b_high, b_mid, b_pair, o_high, o_mid, o_one, o_zero, dq0, dq12, dq3 = run_grads(
        meta, own_lists, before_lists, qs, gs, own_k, own_v, before_k, before_v, all_stats
    )

    b_near = swap(b_high, 1)
    o_near = swap(o_high, 1)
    e12 = swap(dq12, NZ)
    b_far = swap(add_low(b_mid, b_near[2 * one :]), 2)
    back = across(add_low(b_pair, b_near[: 2 * one], b_far), -1)
    o_far = swap(add_low(o_mid, o_near[2 * one :]), 2)
    dq3 = add_low(dq3, e12[BLOCK:])
    e3 = swap(dq3, 3 * NZ)
    o_four = swap(add_low(o_one, o_near[one : 2 * one], o_far[one:], back[one:]), 4)
    grad_queries = add_low(dq0, e12[:BLOCK], e3)
    totals = add_low(o_zero, o_near[:one], o_far[:one], back[:one], o_four)
    return grad_queries, totals[:BLOCK], totals[BLOCK:]


def solution(mesh):
    rows = P(("outer", "inner"), None)
    return jax.shard_map(
        shards,
        mesh=mesh,
        in_specs=(rows, rows, rows, rows, P(), P()),
        out_specs=(rows, rows, rows),
        check_vma=False,
    )
```

```python
import functools

import jax
import jax.numpy as jnp
from jax import lax
from jax.experimental import pallas as pl
from jax.experimental.pallas import tpu as pltpu
from jax.sharding import PartitionSpec as P

BLOCK = 128
HD = 128
HEADS = 8
ROWS = HEADS * BLOCK
GROUP = 32
BLOCKS = 512
FAR = 4
STATS = 16
LIST = 16
EVERY = 32
NY = 4
NZ = 8
CHUNK = 256
NEG = -1e30
SCALE = HD**-0.5
SCALE2 = SCALE * 1.4426950408889634
VMEM_LIMIT = 40 * 1024 * 1024


def dot_nt(a, b):
    return lax.dot_general(a, b, (((1,), (1,)), ((), ())), preferred_element_type=jnp.float32)


def dot_nn(a, b):
    return lax.dot_general(a, b, (((1,), (0,)), ((), ())), preferred_element_type=jnp.float32)


def dot_tn(a, b):
    return lax.dot_general(a, b, (((0,), (0,)), ((), ())), preferred_element_type=jnp.float32)


def stack_heads(refs, qs, gs):
    for r, ref in enumerate(refs):
        for h in range(HEADS):
            to = r * ROWS + h * BLOCK
            qs[to : to + BLOCK, :] = ref[0:BLOCK, h * HD : (h + 1) * HD]
            gs[to : to + BLOCK, :] = ref[BLOCK : 2 * BLOCK, h * HD : (h + 1) * HD]


def place(low, high, ks, vs, base):
    for s in range(NZ):
        ref, lo, to = (low, high)[s // 4], (s % 4) * 2 * BLOCK, (base + s) * BLOCK
        ks[to : to + BLOCK, :] = ref[lo : lo + BLOCK, :]
        vs[to : to + BLOCK, :] = ref[lo + BLOCK : lo + 2 * BLOCK, :]


def list_pairs(meta, before, lists):
    outer, inner = meta[2 * BLOCKS], meta[2 * BLOCKS + 1]
    q_at = [meta[BLOCKS + outer * GROUP + (inner ^ (r * NZ))] for r in range(NY)]
    q_doc = [meta[at] for at in q_at]
    k_at, k_doc = [], []
    for s in range(NZ):
        flip = ((s & 1) << 2) | (s & 2) | ((s >> 2) & 1)
        if before:
            far = jnp.where(outer % 2 == 0, FAR, 0)
            at = meta[BLOCKS + jnp.maximum(outer - 1, 0) * GROUP + (inner ^ flip ^ far)]
            doc = jnp.where(outer > 0, meta[at], -1)
        else:
            at = meta[BLOCKS + outer * GROUP + (inner ^ flip)]
            doc = meta[at]
        k_at.append(at)
        k_doc.append(doc)
    for r in range(NY):
        count = jnp.int32(0)
        for s in range(NZ):
            if not before and r == 0 and s == 0:
                continue
            sees = q_doc[r] == k_doc[s]
            if not before:
                sees = sees & (k_at[s] < q_at[r])
            lists[r * LIST + count] = jnp.int32(s + NZ if before else s)
            count = count + sees.astype(jnp.int32)
        for i in range(4):
            lists[r * LIST + count + i] = jnp.int32(0)
        lists[r * LIST + LIST - 1] = count


def join_lists(first, second, every):
    for r in range(NY):
        at, more = first[r * LIST + LIST - 1], second[r * LIST + LIST - 1]
        for i in range(NZ):
            every[r * EVERY + i] = first[r * LIST + i]
        for i in range(NZ + 1):
            every[r * EVERY + at + i] = jnp.where(i < more, second[r * LIST + i], 0)
        for i in range(4):
            every[r * EVERY + at + more + i] = jnp.int32(0)
        every[r * EVERY + EVERY - 1] = at + more


def diagonal_mask():
    k_at = lax.broadcasted_iota(jnp.int32, (BLOCK, CHUNK), 0)
    q_at = lax.broadcasted_iota(jnp.int32, (BLOCK, CHUNK), 1) % BLOCK
    return k_at <= q_at


def for_quads(diagonal, lists, stride, pair):
    if diagonal:
        pair(0, (0,), (0.0,), True)

    @pl.loop(0, NY)
    def _(r):
        count = lists[r * stride + stride - 1]
        quads = (count + 1) // 4

        def step(width, at):
            slots = [lists[r * stride + at + i] for i in range(width)]
            biases = [jnp.where(at + i < count, 0.0, -NEG) for i in range(width)]
            pair(r, slots, biases, False)

        @pl.loop(0, quads)
        def _(j):
            step(4, 4 * j)

        @pl.loop(0, (count - 4 * quads + 1) // 2)
        def _(j):
            step(2, 4 * quads + 2 * j)


def rows_of(ref, slots):
    return jnp.concatenate([ref[pl.ds(s * BLOCK, BLOCK), :] for s in slots], axis=0)


def stats_kernel(before, *refs):
    if before:
        meta, low, high, qs, gs, earlier, own_k, own_v, own_lists, stats, ks, vs, lists, every = refs
        stats[...] = earlier[...]
        ks[0 : NZ * BLOCK, :] = own_k[...]
        vs[0 : NZ * BLOCK, :] = own_v[...]
    else:
        meta, low, high, *qg, stats, ks, vs, lists, qs, gs = refs
        stack_heads(qg, qs, gs)
        stats[0:NY, :] = jnp.full((NY, ROWS), NEG, jnp.float32)
        stats[NY:STATS, :] = jnp.zeros((STATS - NY, ROWS), jnp.float32)
    list_pairs(meta, before, lists)
    if before:
        join_lists(own_lists, lists, every)
    place(low, high, ks, vs, NZ if before else 0)

    def pair(r, slots, biases, diagonal):
        key, value = rows_of(ks, slots), rows_of(vs, slots)
        for c in range(ROWS // CHUNK):
            rows = pl.ds(r * ROWS + c * CHUNK, CHUNK)
            cols = pl.ds(c * CHUNK, CHUNK)
            scores = dot_nt(key, qs[rows, :]) * SCALE2
            dprob = dot_nt(value, gs[rows, :])
            if diagonal:
                scores = jnp.where(diagonal_mask(), scores, NEG)
            top = stats[pl.ds(r, 1), cols]
            new_top = top
            for i, less in enumerate(biases):
                part = scores[i * BLOCK : (i + 1) * BLOCK]
                new_top = jnp.maximum(new_top, jnp.max(part, axis=0, keepdims=True) - less)
            factor = jnp.exp2(top - new_top)
            total = stats[pl.ds(NY + r, 1), cols] * factor
            product = stats[pl.ds(2 * NY + r, 1), cols] * factor
            for i, less in enumerate(biases):
                half = slice(i * BLOCK, (i + 1) * BLOCK)
                weights = jnp.exp2(scores[half] - (new_top + less))
                total = total + jnp.sum(weights, axis=0, keepdims=True)
                product = product + jnp.sum(weights * dprob[half], axis=0, keepdims=True)
            stats[pl.ds(r, 1), cols] = new_top
            stats[pl.ds(NY + r, 1), cols] = total
            stats[pl.ds(2 * NY + r, 1), cols] = product

    for_quads(not before, lists, LIST, pair)


def grads_kernel(meta, every, qs, gs, ks, vs, stats, *rest):
    b_high, b_mid, b_pair, o_high, o_mid, o_one, o_zero, dq0, dq12, dq3 = rest[:10]
    lse, delta, w_low, d_low, dk, dv, dq = rest[10:]
    dk[...] = jnp.zeros_like(dk)
    dv[...] = jnp.zeros_like(dv)
    dq[...] = jnp.zeros_like(dq)
    me = meta[2 * BLOCKS + 1] // NZ
    for r in range(NY):
        tops, sums, products = [], [], []
        for y in range(NY):
            at = STATS * y + (y ^ me ^ r)
            tops.append(stats[pl.ds(at, 1), :])
            sums.append(stats[pl.ds(at + NY, 1), :])
            products.append(stats[pl.ds(at + 2 * NY, 1), :])
        top = functools.reduce(jnp.maximum, tops)
        factors = [jnp.exp2(t - top) for t in tops]
        total = sum(x * f for x, f in zip(sums, factors))
        product = sum(x * f for x, f in zip(products, factors))
        lse[r : r + 1, :] = top + jnp.log2(total)
        delta[r : r + 1, :] = product / total

    def pair(r, slots, biases, diagonal):
        key, value = rows_of(ks, slots), rows_of(vs, slots)
        count = len(slots) * BLOCK
        for c in range(ROWS // CHUNK):
            rows = pl.ds(r * ROWS + c * CHUNK, CHUNK)
            cols = pl.ds(c * CHUNK, CHUNK)
            scores = dot_nt(key, qs[rows, :]) * SCALE2
            dprob = dot_nt(value, gs[rows, :])
            for i, less in enumerate(biases):
                half = slice(i * BLOCK, (i + 1) * BLOCK)
                probs = jnp.exp2(scores[half] - (lse[pl.ds(r, 1), cols] + less))
                if diagonal:
                    probs = jnp.where(diagonal_mask(), probs, 0.0)
                w_low[half, cols] = probs.astype(jnp.bfloat16)
                dscore = probs * (dprob[half] - delta[pl.ds(r, 1), cols])
                d_low[half, cols] = dscore.astype(jnp.bfloat16)
        rows = pl.ds(r * ROWS, ROWS)
        dk_part = dot_nn(d_low[0:count, :], qs[rows, :])
        dv_part = dot_nn(w_low[0:count, :], gs[rows, :])
        for i, s in enumerate(slots):
            half = slice(i * BLOCK, (i + 1) * BLOCK)
            dk[pl.ds(s * BLOCK, BLOCK), :] += dk_part[half]
            dv[pl.ds(s * BLOCK, BLOCK), :] += dv_part[half]
        dq[pl.ds(r * HD, HD), :] += dot_tn(key, d_low[0:count, :])

    for_quads(True, every, EVERY, pair)

    def write(slots, out, at):
        for s in slots:
            rows = slice(s * BLOCK, (s + 1) * BLOCK)
            out[at : at + BLOCK, :] = (dk[rows, :] * SCALE).astype(jnp.bfloat16)
            out[at + BLOCK : at + 2 * BLOCK, :] = dv[rows, :].astype(jnp.bfloat16)
            at += 2 * BLOCK

    write((NZ + 4, NZ + 5, NZ + 6, NZ + 7), b_high, 0)
    write((NZ + 2, NZ + 3), b_mid, 0)
    write((NZ, NZ + 1), b_pair, 0)
    write((4, 5, 6, 7), o_high, 0)
    write((2, 3), o_mid, 0)
    write((1,), o_one, 0)
    write((0,), o_zero, 0)
    for r, (out, at) in enumerate(((dq0, 0), (dq12, 0), (dq12, BLOCK), (dq3, 0))):
        for h in range(HEADS):
            part = dq[r * HD : (r + 1) * HD, h * BLOCK : (h + 1) * BLOCK] * SCALE
            out[at : at + BLOCK, h * HD : (h + 1) * HD] = part.astype(jnp.bfloat16).T


def smem():
    return pl.BlockSpec(memory_space=pltpu.SMEM)


def vmem():
    return pl.BlockSpec(memory_space=pltpu.VMEM)


def cost(matmuls, pairs):
    return pl.CostEstimate(
        flops=matmuls * pairs * 2 * ROWS * BLOCK * HD,
        bytes_accessed=4 * 1024 * 1024,
        transcendentals=pairs * ROWS * BLOCK,
    )


def run_stats(before, *args):
    blocks = jax.ShapeDtypeStruct(((2 if before else 1) * NZ * BLOCK, HD), jnp.bfloat16)
    outs = [
        jax.ShapeDtypeStruct((STATS, ROWS), jnp.float32),
        blocks,
        blocks,
        jax.ShapeDtypeStruct((NY * LIST,), jnp.int32),
    ]
    in_specs = [smem()] + [vmem()] * (len(args) - 1)
    specs = [vmem()] * 3 + [smem()]
    if before:
        outs.append(jax.ShapeDtypeStruct((NY * EVERY,), jnp.int32))
        specs.append(smem())
        in_specs[-1] = smem()
    else:
        outs += [jax.ShapeDtypeStruct((NY * ROWS, HD), jnp.bfloat16)] * 2
        specs += [vmem()] * 2
    return pl.pallas_call(
        functools.partial(stats_kernel, before),
        out_shape=outs,
        in_specs=in_specs,
        out_specs=specs,
        compiler_params=pltpu.CompilerParams(vmem_limit_bytes=VMEM_LIMIT),
        cost_estimate=cost(2, 10),
    )(*args)


def run_grads(*args):
    outs = [jax.ShapeDtypeStruct((n * 2 * BLOCK, HD), jnp.bfloat16) for n in (4, 2, 2, 4, 2, 1, 1)]
    outs += [jax.ShapeDtypeStruct((n * BLOCK, HEADS * HD), jnp.bfloat16) for n in (1, 2, 1)]
    return pl.pallas_call(
        grads_kernel,
        out_shape=outs,
        in_specs=[smem()] * 2 + [vmem()] * (len(args) - 2),
        out_specs=[vmem()] * len(outs),
        scratch_shapes=[
            pltpu.VMEM((NY, ROWS), jnp.float32),
            pltpu.VMEM((NY, ROWS), jnp.float32),
            pltpu.VMEM((4 * BLOCK, ROWS), jnp.bfloat16),
            pltpu.VMEM((4 * BLOCK, ROWS), jnp.bfloat16),
            pltpu.VMEM((2 * NZ * BLOCK, HD), jnp.float32),
            pltpu.VMEM((2 * NZ * BLOCK, HD), jnp.float32),
            pltpu.VMEM((NY * HD, ROWS), jnp.float32),
        ],
        compiler_params=pltpu.CompilerParams(vmem_limit_bytes=VMEM_LIMIT),
        cost_estimate=cost(5, 20),
    )(*args)


def swap(array, flip):
    return lax.ppermute(array, "inner", [(i, i ^ flip) for i in range(GROUP)])


def across(array, by):
    outer = lax.axis_size("outer")
    pairs = [
        (o * GROUP + i, (o + by) * GROUP + (i ^ (0 if max(o, o + by) % 2 else FAR)))
        for o in range(outer)
        if 0 <= o + by < outer
        for i in range(GROUP)
    ]
    return lax.ppermute(array, ("outer", "inner"), pairs)


def add_low(*terms):
    total = terms[0].astype(jnp.float32)
    for term in terms[1:]:
        total = total + term.astype(jnp.float32)
    return total.astype(jnp.bfloat16)


def shards(queries, keys, values, grad_out, doc_ids, block_order):
    one = 2 * BLOCK
    ids = jnp.stack([lax.axis_index("outer"), lax.axis_index("inner")]).astype(jnp.int32)
    meta = jnp.concatenate([doc_ids, block_order, ids])
    own = jnp.concatenate([keys, values], axis=0)
    qg0 = jnp.concatenate([queries, grad_out], axis=0)

    own4 = swap(own, 4)
    qg_later, _ = lax.optimization_barrier((qg0, own4))
    qg1 = swap(qg0, NZ)
    qg3 = swap(qg_later, 3 * NZ)
    qg2 = swap(qg_later, 2 * NZ)
    own_pair = jnp.concatenate([own, own4], axis=0)
    before_pair = across(own_pair, 1)
    own_low = jnp.concatenate([own_pair, swap(own_pair, 2)], axis=0)
    own_high = swap(own_low, 1)
    before_low = jnp.concatenate([before_pair, swap(before_pair, 2)], axis=0)
    before_low, qg1, qg2 = lax.optimization_barrier((before_low, qg1, qg2))
    before_high = swap(before_low, 1)

    stats, own_k, own_v, own_lists, qs, gs = run_stats(
        False, meta, own_low, own_high, qg0, qg1, qg2, qg3
    )
    stats, ks, vs, _, every = run_stats(
        True, meta, before_low, before_high, qs, gs, stats, own_k, own_v, own_lists
    )
    along_y = [[y * NZ + z for y in range(NY)] for z in range(NZ)]
    all_stats = lax.all_gather(stats, "inner", axis=0, tiled=True, axis_index_groups=along_y)
    b_high, b_mid, b_pair, o_high, o_mid, o_one, o_zero, dq0, dq12, dq3 = run_grads(
        meta, every, qs, gs, ks, vs, all_stats
    )

    b_near = swap(b_high, 1)
    o_near = swap(o_high, 1)
    e12 = swap(dq12, NZ)
    b_far = swap(add_low(b_mid, b_near[2 * one :]), 2)
    back = across(add_low(b_pair, b_near[: 2 * one], b_far), -1)
    o_far = swap(add_low(o_mid, o_near[2 * one :]), 2)
    e3 = swap(add_low(dq3, e12[BLOCK:]), 3 * NZ)
    o_four = swap(add_low(o_one, o_near[one : 2 * one], o_far[one:], back[one:]), 4)
    grad_queries = add_low(dq0, e12[:BLOCK], e3)
    terms = (o_zero, o_near[:one], o_far[:one], back[:one], o_four)
    grad_keys = add_low(*[term[:BLOCK] for term in terms])
    grad_values = add_low(*[term[BLOCK:] for term in terms])
    return grad_queries, grad_keys, grad_values


def solution(mesh):
    rows = P(("outer", "inner"), None)
    return jax.shard_map(
        shards,
        mesh=mesh,
        in_specs=(rows, rows, rows, rows, P(), P()),
        out_specs=(rows, rows, rows),
        check_vma=False,
    )
```

```python
import functools

import jax
import jax.numpy as jnp
from jax import lax
from jax.experimental import pallas as pl
from jax.experimental.pallas import tpu as pltpu
from jax.sharding import PartitionSpec as P

BLOCK = 128
HD = 128
HEADS = 8
ROWS = HEADS * BLOCK
GROUP = 32
BLOCKS = 512
FAR = 4
STATS = 16
LIST = 16
EVERY = 32
NY = 4
NZ = 8
CHUNK = 256
NEG = -1e30
SCALE = HD**-0.5
SCALE2 = SCALE * 1.4426950408889634
VMEM_LIMIT = 40 * 1024 * 1024


def dot_nt(a, b):
    return lax.dot_general(a, b, (((1,), (1,)), ((), ())), preferred_element_type=jnp.float32)


def dot_nn(a, b):
    return lax.dot_general(a, b, (((1,), (0,)), ((), ())), preferred_element_type=jnp.float32)


def dot_tn(a, b):
    return lax.dot_general(a, b, (((0,), (0,)), ((), ())), preferred_element_type=jnp.float32)


def stack_heads(refs, qs, gs):
    for r, ref in enumerate(refs):
        for h in range(HEADS):
            to = r * ROWS + h * BLOCK
            qs[to : to + BLOCK, :] = ref[0:BLOCK, h * HD : (h + 1) * HD]
            gs[to : to + BLOCK, :] = ref[BLOCK : 2 * BLOCK, h * HD : (h + 1) * HD]


def place(low, high, ks, vs, base):
    for s in range(NZ):
        ref, lo, to = (low, high)[s // 4], (s % 4) * 2 * BLOCK, (base + s) * BLOCK
        ks[to : to + BLOCK, :] = ref[lo : lo + BLOCK, :]
        vs[to : to + BLOCK, :] = ref[lo + BLOCK : lo + 2 * BLOCK, :]


def list_pairs(meta, before, lists):
    outer, inner = meta[2 * BLOCKS], meta[2 * BLOCKS + 1]
    q_at = [meta[BLOCKS + outer * GROUP + (inner ^ (r * NZ))] for r in range(NY)]
    q_doc = [meta[at] for at in q_at]
    k_at, k_doc = [], []
    for s in range(NZ):
        flip = ((s & 1) << 2) | (s & 2) | ((s >> 2) & 1)
        if before:
            far = jnp.where(outer % 2 == 0, FAR, 0)
            at = meta[BLOCKS + jnp.maximum(outer - 1, 0) * GROUP + (inner ^ flip ^ far)]
            doc = jnp.where(outer > 0, meta[at], -1)
        else:
            at = meta[BLOCKS + outer * GROUP + (inner ^ flip)]
            doc = meta[at]
        k_at.append(at)
        k_doc.append(doc)
    for r in range(NY):
        count = jnp.int32(0)
        for s in range(NZ):
            if not before and r == 0 and s == 0:
                continue
            sees = q_doc[r] == k_doc[s]
            if not before:
                sees = sees & (k_at[s] < q_at[r])
            lists[r * LIST + count] = jnp.int32(s + NZ if before else s)
            count = count + sees.astype(jnp.int32)
        for i in range(4):
            lists[r * LIST + count + i] = jnp.int32(0)
        lists[r * LIST + LIST - 1] = count


def join_lists(first, second, every):
    for r in range(NY):
        at, more = first[r * LIST + LIST - 1], second[r * LIST + LIST - 1]
        for i in range(NZ):
            every[r * EVERY + i] = first[r * LIST + i]
        for i in range(NZ + 1):
            every[r * EVERY + at + i] = jnp.where(i < more, second[r * LIST + i], 0)
        for i in range(4):
            every[r * EVERY + at + more + i] = jnp.int32(0)
        every[r * EVERY + EVERY - 1] = at + more


def diagonal_mask():
    k_at = lax.broadcasted_iota(jnp.int32, (BLOCK, CHUNK), 0)
    q_at = lax.broadcasted_iota(jnp.int32, (BLOCK, CHUNK), 1) % BLOCK
    return k_at <= q_at


def for_quads(diagonal, lists, stride, pair):
    if diagonal:
        pair(0, (0,), (0.0,), True)

    @pl.loop(0, NY)
    def _(r):
        count = lists[r * stride + stride - 1]
        quads = (count + 1) // 4

        def step(width, at):
            slots = [lists[r * stride + at + i] for i in range(width)]
            biases = [jnp.where(at + i < count, 0.0, -NEG) for i in range(width)]
            pair(r, slots, biases, False)

        @pl.loop(0, quads)
        def _(j):
            step(4, 4 * j)

        @pl.loop(0, (count - 4 * quads + 1) // 2)
        def _(j):
            step(2, 4 * quads + 2 * j)


def rows_of(ref, slots):
    return jnp.concatenate([ref[pl.ds(s * BLOCK, BLOCK), :] for s in slots], axis=0)


def stats_kernel(before, *refs):
    if before:
        meta, low, high, qs, gs, earlier, own_k, own_v, own_lists, stats, ks, vs, lists, every = refs
        stats[...] = earlier[...]
        ks[0 : NZ * BLOCK, :] = own_k[...]
        vs[0 : NZ * BLOCK, :] = own_v[...]
    else:
        meta, low, high, *qg, stats, ks, vs, lists, qs, gs = refs
        stack_heads(qg, qs, gs)
        stats[0:NY, :] = jnp.full((NY, ROWS), NEG, jnp.float32)
        stats[NY:STATS, :] = jnp.zeros((STATS - NY, ROWS), jnp.float32)
    list_pairs(meta, before, lists)
    if before:
        join_lists(own_lists, lists, every)
    place(low, high, ks, vs, NZ if before else 0)

    def pair(r, slots, biases, diagonal):
        key, value = rows_of(ks, slots), rows_of(vs, slots)
        for c in range(ROWS // CHUNK):
            rows = pl.ds(r * ROWS + c * CHUNK, CHUNK)
            cols = pl.ds(c * CHUNK, CHUNK)
            scores = dot_nt(key, qs[rows, :]) * SCALE2
            dprob = dot_nt(value, gs[rows, :])
            if diagonal:
                scores = jnp.where(diagonal_mask(), scores, NEG)
            top = stats[pl.ds(r, 1), cols]
            new_top = top
            for i, less in enumerate(biases):
                part = scores[i * BLOCK : (i + 1) * BLOCK]
                new_top = jnp.maximum(new_top, jnp.max(part, axis=0, keepdims=True) - less)
            factor = jnp.exp2(top - new_top)
            total = stats[pl.ds(NY + r, 1), cols] * factor
            product = stats[pl.ds(2 * NY + r, 1), cols] * factor
            for i, less in enumerate(biases):
                half = slice(i * BLOCK, (i + 1) * BLOCK)
                weights = jnp.exp2(scores[half] - (new_top + less))
                total = total + jnp.sum(weights, axis=0, keepdims=True)
                product = product + jnp.sum(weights * dprob[half], axis=0, keepdims=True)
            stats[pl.ds(r, 1), cols] = new_top
            stats[pl.ds(NY + r, 1), cols] = total
            stats[pl.ds(2 * NY + r, 1), cols] = product

    for_quads(not before, lists, LIST, pair)


def grads_kernel(meta, every, qs, gs, ks, vs, stats, *rest):
    b_high, b_mid, b_pair, o_high, o_mid, o_one, o_zero, dq0, dq12, dq3 = rest[:10]
    lse, delta, w_low, d_low, dk, dv, dq = rest[10:]
    dk[...] = jnp.zeros_like(dk)
    dv[...] = jnp.zeros_like(dv)
    dq[...] = jnp.zeros_like(dq)
    me = meta[2 * BLOCKS + 1] // NZ
    for r in range(NY):
        tops, sums, products = [], [], []
        for y in range(NY):
            at = STATS * y + (y ^ me ^ r)
            tops.append(stats[pl.ds(at, 1), :])
            sums.append(stats[pl.ds(at + NY, 1), :])
            products.append(stats[pl.ds(at + 2 * NY, 1), :])
        top = functools.reduce(jnp.maximum, tops)
        factors = [jnp.exp2(t - top) for t in tops]
        total = sum(x * f for x, f in zip(sums, factors))
        product = sum(x * f for x, f in zip(products, factors))
        lse[r : r + 1, :] = top + jnp.log2(total)
        delta[r : r + 1, :] = product / total

    def pair(r, slots, biases, diagonal):
        key, value = rows_of(ks, slots), rows_of(vs, slots)
        count = len(slots) * BLOCK
        for c in range(ROWS // CHUNK):
            rows = pl.ds(r * ROWS + c * CHUNK, CHUNK)
            cols = pl.ds(c * CHUNK, CHUNK)
            scores = dot_nt(key, qs[rows, :]) * SCALE2
            dprob = dot_nt(value, gs[rows, :])
            for i, less in enumerate(biases):
                half = slice(i * BLOCK, (i + 1) * BLOCK)
                probs = jnp.exp2(scores[half] - (lse[pl.ds(r, 1), cols] + less))
                if diagonal:
                    probs = jnp.where(diagonal_mask(), probs, 0.0)
                w_low[half, cols] = probs.astype(jnp.bfloat16)
                dscore = probs * (dprob[half] - delta[pl.ds(r, 1), cols])
                d_low[half, cols] = dscore.astype(jnp.bfloat16)
        rows = pl.ds(r * ROWS, ROWS)
        dk_part = dot_nn(d_low[0:count, :], qs[rows, :])
        dv_part = dot_nn(w_low[0:count, :], gs[rows, :])
        for i, s in enumerate(slots):
            half = slice(i * BLOCK, (i + 1) * BLOCK)
            dk[pl.ds(s * BLOCK, BLOCK), :] += dk_part[half]
            dv[pl.ds(s * BLOCK, BLOCK), :] += dv_part[half]
        dq[pl.ds(r * HD, HD), :] += dot_tn(key, d_low[0:count, :])

    for_quads(True, every, EVERY, pair)

    def write(slots, out, at):
        for s in slots:
            rows = slice(s * BLOCK, (s + 1) * BLOCK)
            out[at : at + BLOCK, :] = (dk[rows, :] * SCALE).astype(jnp.bfloat16)
            out[at + BLOCK : at + 2 * BLOCK, :] = dv[rows, :].astype(jnp.bfloat16)
            at += 2 * BLOCK

    write((NZ + 4, NZ + 5, NZ + 6, NZ + 7), b_high, 0)
    write((NZ + 2, NZ + 3), b_mid, 0)
    write((NZ, NZ + 1), b_pair, 0)
    write((4, 5, 6, 7), o_high, 0)
    write((2, 3), o_mid, 0)
    write((1,), o_one, 0)
    write((0,), o_zero, 0)
    for r, (out, at) in enumerate(((dq0, 0), (dq12, 0), (dq12, BLOCK), (dq3, 0))):
        for h in range(HEADS):
            part = dq[r * HD : (r + 1) * HD, h * BLOCK : (h + 1) * BLOCK] * SCALE
            out[at : at + BLOCK, h * HD : (h + 1) * HD] = part.astype(jnp.bfloat16).T


def smem():
    return pl.BlockSpec(memory_space=pltpu.SMEM)


def vmem():
    return pl.BlockSpec(memory_space=pltpu.VMEM)


def cost(matmuls, pairs):
    return pl.CostEstimate(
        flops=matmuls * pairs * 2 * ROWS * BLOCK * HD,
        bytes_accessed=4 * 1024 * 1024,
        transcendentals=pairs * ROWS * BLOCK,
    )


def run_stats(before, *args):
    blocks = jax.ShapeDtypeStruct(((2 if before else 1) * NZ * BLOCK, HD), jnp.bfloat16)
    outs = [
        jax.ShapeDtypeStruct((STATS, ROWS), jnp.float32),
        blocks,
        blocks,
        jax.ShapeDtypeStruct((NY * LIST,), jnp.int32),
    ]
    in_specs = [smem()] + [vmem()] * (len(args) - 1)
    specs = [vmem()] * 3 + [smem()]
    if before:
        outs.append(jax.ShapeDtypeStruct((NY * EVERY,), jnp.int32))
        specs.append(smem())
        in_specs[-1] = smem()
    else:
        outs += [jax.ShapeDtypeStruct((NY * ROWS, HD), jnp.bfloat16)] * 2
        specs += [vmem()] * 2
    return pl.pallas_call(
        functools.partial(stats_kernel, before),
        out_shape=outs,
        in_specs=in_specs,
        out_specs=specs,
        compiler_params=pltpu.CompilerParams(vmem_limit_bytes=VMEM_LIMIT),
        cost_estimate=cost(2, 10),
    )(*args)


def run_grads(*args):
    outs = [jax.ShapeDtypeStruct((n * 2 * BLOCK, HD), jnp.bfloat16) for n in (4, 2, 2, 4, 2, 1, 1)]
    outs += [jax.ShapeDtypeStruct((n * BLOCK, HEADS * HD), jnp.bfloat16) for n in (1, 2, 1)]
    return pl.pallas_call(
        grads_kernel,
        out_shape=outs,
        in_specs=[smem()] * 2 + [vmem()] * (len(args) - 2),
        out_specs=[vmem()] * len(outs),
        scratch_shapes=[
            pltpu.VMEM((NY, ROWS), jnp.float32),
            pltpu.VMEM((NY, ROWS), jnp.float32),
            pltpu.VMEM((4 * BLOCK, ROWS), jnp.bfloat16),
            pltpu.VMEM((4 * BLOCK, ROWS), jnp.bfloat16),
            pltpu.VMEM((2 * NZ * BLOCK, HD), jnp.float32),
            pltpu.VMEM((2 * NZ * BLOCK, HD), jnp.float32),
            pltpu.VMEM((NY * HD, ROWS), jnp.float32),
        ],
        compiler_params=pltpu.CompilerParams(vmem_limit_bytes=VMEM_LIMIT),
        cost_estimate=cost(5, 20),
    )(*args)


def swap(array, flip):
    return lax.ppermute(array, "inner", [(i, i ^ flip) for i in range(GROUP)])


def across(array, by):
    outer = lax.axis_size("outer")
    pairs = [
        (o * GROUP + i, (o + by) * GROUP + (i ^ (0 if max(o, o + by) % 2 else FAR)))
        for o in range(outer)
        if 0 <= o + by < outer
        for i in range(GROUP)
    ]
    return lax.ppermute(array, ("outer", "inner"), pairs)


def add_low(*terms):
    total = terms[0].astype(jnp.float32)
    for term in terms[1:]:
        total = total + term.astype(jnp.float32)
    return total.astype(jnp.bfloat16)


def shards(queries, keys, values, grad_out, doc_ids, block_order):
    one = 2 * BLOCK
    ids = jnp.stack([lax.axis_index("outer"), lax.axis_index("inner")]).astype(jnp.int32)
    meta = jnp.concatenate([doc_ids, block_order, ids])
    own = jnp.concatenate([keys, values], axis=0)
    qg0 = jnp.concatenate([queries, grad_out], axis=0)

    own4 = swap(own, 4)
    qg_later, _ = lax.optimization_barrier((qg0, own4))
    qg1 = swap(qg0, NZ)
    qg3 = swap(qg_later, 3 * NZ)
    qg2 = swap(qg_later, 2 * NZ)
    own_pair = jnp.concatenate([own, own4], axis=0)
    before_pair = across(own_pair, 1)
    own_low = jnp.concatenate([own_pair, swap(own_pair, 2)], axis=0)
    own_high = swap(own_low, 1)
    before_low = jnp.concatenate([before_pair, swap(before_pair, 2)], axis=0)
    before_low, qg1, qg3 = lax.optimization_barrier((before_low, qg1, qg3))
    before_high = swap(before_low, 1)

    stats, own_k, own_v, own_lists, qs, gs = run_stats(
        False, meta, own_low, own_high, qg0, qg1, qg2, qg3
    )
    stats, ks, vs, _, every = run_stats(
        True, meta, before_low, before_high, qs, gs, stats, own_k, own_v, own_lists
    )
    along_y = [[y * NZ + z for y in range(NY)] for z in range(NZ)]
    all_stats = lax.all_gather(stats, "inner", axis=0, tiled=True, axis_index_groups=along_y)
    b_high, b_mid, b_pair, o_high, o_mid, o_one, o_zero, dq0, dq12, dq3 = run_grads(
        meta, every, qs, gs, ks, vs, all_stats
    )

    b_near = swap(b_high, 1)
    o_near = swap(o_high, 1)
    e12 = swap(dq12, NZ)
    b_far = swap(add_low(b_mid, b_near[2 * one :]), 2)
    back = across(add_low(b_pair, b_near[: 2 * one], b_far), -1)
    o_far = swap(add_low(o_mid, o_near[2 * one :]), 2)
    e3 = swap(add_low(dq3, e12[BLOCK:]), 3 * NZ)
    o_four = swap(add_low(o_one, o_near[one : 2 * one], o_far[one:], back[one:]), 4)
    o_four, e3 = lax.optimization_barrier((o_four, e3))
    grad_queries = add_low(dq0, e12[:BLOCK], e3)
    terms = (o_zero, o_near[:one], o_far[:one], back[:one], o_four)
    grad_keys = add_low(*[term[:BLOCK] for term in terms])
    grad_values = add_low(*[term[BLOCK:] for term in terms])
    return grad_queries, grad_keys, grad_values


def solution(mesh):
    rows = P(("outer", "inner"), None)
    return jax.shard_map(
        shards,
        mesh=mesh,
        in_specs=(rows, rows, rows, rows, P(), P()),
        out_specs=(rows, rows, rows),
        check_vma=False,
    )
```

```python
import functools

import jax
import jax.numpy as jnp
from jax import lax
from jax.experimental import pallas as pl
from jax.experimental.pallas import tpu as pltpu
from jax.sharding import PartitionSpec as P

BLOCK = 128
HD = 128
HEADS = 8
ROWS = HEADS * BLOCK
GROUP = 32
BLOCKS = 512
FAR = 4
STATS = 16
LIST = 16
EVERY = 32
NY = 4
NZ = 8
CHUNK = 256
NEG = -1e30
SCALE = HD**-0.5
SCALE2 = SCALE * 1.4426950408889634
VMEM_LIMIT = 40 * 1024 * 1024


def dot_nt(a, b):
    return lax.dot_general(a, b, (((1,), (1,)), ((), ())), preferred_element_type=jnp.float32)


def dot_nn(a, b):
    return lax.dot_general(a, b, (((1,), (0,)), ((), ())), preferred_element_type=jnp.float32)


def dot_tn(a, b):
    return lax.dot_general(a, b, (((0,), (0,)), ((), ())), preferred_element_type=jnp.float32)


def stack_heads(refs, qs, gs):
    for r, ref in enumerate(refs):
        for h in range(HEADS):
            to = r * ROWS + h * BLOCK
            qs[to : to + BLOCK, :] = ref[0:BLOCK, h * HD : (h + 1) * HD]
            gs[to : to + BLOCK, :] = ref[BLOCK : 2 * BLOCK, h * HD : (h + 1) * HD]


def place(low, high, ks, vs, base):
    for s in range(NZ):
        ref, lo, to = (low, high)[s // 4], (s % 4) * 2 * BLOCK, (base + s) * BLOCK
        ks[to : to + BLOCK, :] = ref[lo : lo + BLOCK, :]
        vs[to : to + BLOCK, :] = ref[lo + BLOCK : lo + 2 * BLOCK, :]


def list_pairs(meta, before, lists):
    outer, inner = meta[2 * BLOCKS], meta[2 * BLOCKS + 1]
    q_at = [meta[BLOCKS + outer * GROUP + (inner ^ (r * NZ))] for r in range(NY)]
    q_doc = [meta[at] for at in q_at]
    k_at, k_doc = [], []
    for s in range(NZ):
        flip = ((s & 1) << 2) | (s & 2) | ((s >> 2) & 1)
        if before:
            far = jnp.where(outer % 2 == 0, FAR, 0)
            at = meta[BLOCKS + jnp.maximum(outer - 1, 0) * GROUP + (inner ^ flip ^ far)]
            doc = jnp.where(outer > 0, meta[at], -1)
        else:
            at = meta[BLOCKS + outer * GROUP + (inner ^ flip)]
            doc = meta[at]
        k_at.append(at)
        k_doc.append(doc)
    for r in range(NY):
        count = jnp.int32(0)
        for s in range(NZ):
            if not before and r == 0 and s == 0:
                continue
            sees = q_doc[r] == k_doc[s]
            if not before:
                sees = sees & (k_at[s] < q_at[r])
            lists[r * LIST + count] = jnp.int32(s + NZ if before else s)
            count = count + sees.astype(jnp.int32)
        for i in range(4):
            lists[r * LIST + count + i] = jnp.int32(0)
        lists[r * LIST + LIST - 1] = count


def join_lists(first, second, every):
    for r in range(NY):
        at, more = first[r * LIST + LIST - 1], second[r * LIST + LIST - 1]
        for i in range(NZ):
            every[r * EVERY + i] = first[r * LIST + i]
        for i in range(NZ + 1):
            every[r * EVERY + at + i] = jnp.where(i < more, second[r * LIST + i], 0)
        for i in range(4):
            every[r * EVERY + at + more + i] = jnp.int32(0)
        every[r * EVERY + EVERY - 1] = at + more


def diagonal_mask():
    k_at = lax.broadcasted_iota(jnp.int32, (BLOCK, CHUNK), 0)
    q_at = lax.broadcasted_iota(jnp.int32, (BLOCK, CHUNK), 1) % BLOCK
    return k_at <= q_at


def for_quads(diagonal, lists, stride, pair):
    if diagonal:
        pair(0, (0,), (0.0,), True)

    @pl.loop(0, NY)
    def _(r):
        count = lists[r * stride + stride - 1]
        quads = (count + 1) // 4

        def step(width, at):
            slots = [lists[r * stride + at + i] for i in range(width)]
            biases = [jnp.where(at + i < count, 0.0, -NEG) for i in range(width)]
            pair(r, slots, biases, False)

        @pl.loop(0, quads)
        def _(j):
            step(4, 4 * j)

        @pl.loop(0, (count - 4 * quads + 1) // 2)
        def _(j):
            step(2, 4 * quads + 2 * j)


def rows_of(ref, slots):
    return jnp.concatenate([ref[pl.ds(s * BLOCK, BLOCK), :] for s in slots], axis=0)


def stats_kernel(before, *refs):
    if before:
        meta, low, high, qs, gs, earlier, own_k, own_v, own_lists, stats, ks, vs, lists, every = refs
        stats[...] = earlier[...]
        ks[0 : NZ * BLOCK, :] = own_k[...]
        vs[0 : NZ * BLOCK, :] = own_v[...]
    else:
        meta, low, high, *qg, stats, ks, vs, lists, qs, gs = refs
        stack_heads(qg, qs, gs)
        stats[0:NY, :] = jnp.full((NY, ROWS), NEG, jnp.float32)
        stats[NY:STATS, :] = jnp.zeros((STATS - NY, ROWS), jnp.float32)
    list_pairs(meta, before, lists)
    if before:
        join_lists(own_lists, lists, every)
    place(low, high, ks, vs, NZ if before else 0)

    def pair(r, slots, biases, diagonal):
        key, value = rows_of(ks, slots), rows_of(vs, slots)
        for c in range(ROWS // CHUNK):
            rows = pl.ds(r * ROWS + c * CHUNK, CHUNK)
            cols = pl.ds(c * CHUNK, CHUNK)
            scores = dot_nt(key, qs[rows, :]) * SCALE2
            dprob = dot_nt(value, gs[rows, :])
            if diagonal:
                scores = jnp.where(diagonal_mask(), scores, NEG)
            top = stats[pl.ds(r, 1), cols]
            new_top = top
            for i, less in enumerate(biases):
                part = scores[i * BLOCK : (i + 1) * BLOCK]
                new_top = jnp.maximum(new_top, jnp.max(part, axis=0, keepdims=True) - less)
            factor = jnp.exp2(top - new_top)
            total = stats[pl.ds(NY + r, 1), cols] * factor
            product = stats[pl.ds(2 * NY + r, 1), cols] * factor
            for i, less in enumerate(biases):
                half = slice(i * BLOCK, (i + 1) * BLOCK)
                weights = jnp.exp2(scores[half] - (new_top + less))
                total = total + jnp.sum(weights, axis=0, keepdims=True)
                product = product + jnp.sum(weights * dprob[half], axis=0, keepdims=True)
            stats[pl.ds(r, 1), cols] = new_top
            stats[pl.ds(NY + r, 1), cols] = total
            stats[pl.ds(2 * NY + r, 1), cols] = product

    for_quads(not before, lists, LIST, pair)


def grads_kernel(meta, every, qs, gs, ks, vs, stats, *rest):
    b_high, b_mid, b_pair, o_high, o_mid, o_one, o_zero, dq0, dq12, dq3 = rest[:10]
    lse, delta, w_low, d_low, dk, dv, dq = rest[10:]
    dk[...] = jnp.zeros_like(dk)
    dv[...] = jnp.zeros_like(dv)
    dq[...] = jnp.zeros_like(dq)
    me = meta[2 * BLOCKS + 1] // NZ
    for r in range(NY):
        tops, sums, products = [], [], []
        for y in range(NY):
            at = STATS * y + (y ^ me ^ r)
            tops.append(stats[pl.ds(at, 1), :])
            sums.append(stats[pl.ds(at + NY, 1), :])
            products.append(stats[pl.ds(at + 2 * NY, 1), :])
        top = functools.reduce(jnp.maximum, tops)
        factors = [jnp.exp2(t - top) for t in tops]
        total = sum(x * f for x, f in zip(sums, factors))
        product = sum(x * f for x, f in zip(products, factors))
        lse[r : r + 1, :] = top + jnp.log2(total)
        delta[r : r + 1, :] = product / total

    def pair(r, slots, biases, diagonal):
        key, value = rows_of(ks, slots), rows_of(vs, slots)
        count = len(slots) * BLOCK
        for c in range(ROWS // CHUNK):
            rows = pl.ds(r * ROWS + c * CHUNK, CHUNK)
            cols = pl.ds(c * CHUNK, CHUNK)
            scores = dot_nt(key, qs[rows, :]) * SCALE2
            dprob = dot_nt(value, gs[rows, :])
            for i, less in enumerate(biases):
                half = slice(i * BLOCK, (i + 1) * BLOCK)
                probs = jnp.exp2(scores[half] - (lse[pl.ds(r, 1), cols] + less))
                if diagonal:
                    probs = jnp.where(diagonal_mask(), probs, 0.0)
                w_low[half, cols] = probs.astype(jnp.bfloat16)
                dscore = probs * (dprob[half] - delta[pl.ds(r, 1), cols])
                d_low[half, cols] = dscore.astype(jnp.bfloat16)
        rows = pl.ds(r * ROWS, ROWS)
        dk_part = dot_nn(d_low[0:count, :], qs[rows, :])
        dv_part = dot_nn(w_low[0:count, :], gs[rows, :])
        for i, s in enumerate(slots):
            half = slice(i * BLOCK, (i + 1) * BLOCK)
            dk[pl.ds(s * BLOCK, BLOCK), :] += dk_part[half]
            dv[pl.ds(s * BLOCK, BLOCK), :] += dv_part[half]
        dq[pl.ds(r * HD, HD), :] += dot_tn(key, d_low[0:count, :])

    for_quads(True, every, EVERY, pair)

    def write(slots, out, at):
        for s in slots:
            rows = slice(s * BLOCK, (s + 1) * BLOCK)
            out[at : at + BLOCK, :] = (dk[rows, :] * SCALE).astype(jnp.bfloat16)
            out[at + BLOCK : at + 2 * BLOCK, :] = dv[rows, :].astype(jnp.bfloat16)
            at += 2 * BLOCK

    write((NZ + 4, NZ + 5, NZ + 6, NZ + 7), b_high, 0)
    write((NZ + 2, NZ + 3), b_mid, 0)
    write((NZ, NZ + 1), b_pair, 0)
    write((4, 5, 6, 7), o_high, 0)
    write((2, 3), o_mid, 0)
    write((1,), o_one, 0)
    write((0,), o_zero, 0)
    for r, (out, at) in enumerate(((dq0, 0), (dq12, 0), (dq12, BLOCK), (dq3, 0))):
        for h in range(HEADS):
            part = dq[r * HD : (r + 1) * HD, h * BLOCK : (h + 1) * BLOCK] * SCALE
            out[at : at + BLOCK, h * HD : (h + 1) * HD] = part.astype(jnp.bfloat16).T


def smem():
    return pl.BlockSpec(memory_space=pltpu.SMEM)


def vmem():
    return pl.BlockSpec(memory_space=pltpu.VMEM)


def cost(matmuls, pairs):
    return pl.CostEstimate(
        flops=matmuls * pairs * 2 * ROWS * BLOCK * HD,
        bytes_accessed=4 * 1024 * 1024,
        transcendentals=pairs * ROWS * BLOCK,
    )


def run_stats(before, *args):
    blocks = jax.ShapeDtypeStruct(((2 if before else 1) * NZ * BLOCK, HD), jnp.bfloat16)
    outs = [
        jax.ShapeDtypeStruct((STATS, ROWS), jnp.float32),
        blocks,
        blocks,
        jax.ShapeDtypeStruct((NY * LIST,), jnp.int32),
    ]
    in_specs = [smem()] + [vmem()] * (len(args) - 1)
    specs = [vmem()] * 3 + [smem()]
    if before:
        outs.append(jax.ShapeDtypeStruct((NY * EVERY,), jnp.int32))
        specs.append(smem())
        in_specs[-1] = smem()
    else:
        outs += [jax.ShapeDtypeStruct((NY * ROWS, HD), jnp.bfloat16)] * 2
        specs += [vmem()] * 2
    return pl.pallas_call(
        functools.partial(stats_kernel, before),
        out_shape=outs,
        in_specs=in_specs,
        out_specs=specs,
        compiler_params=pltpu.CompilerParams(vmem_limit_bytes=VMEM_LIMIT),
        cost_estimate=cost(2, 10),
    )(*args)


def run_grads(*args):
    outs = [jax.ShapeDtypeStruct((n * 2 * BLOCK, HD), jnp.bfloat16) for n in (4, 2, 2, 4, 2, 1, 1)]
    outs += [jax.ShapeDtypeStruct((n * BLOCK, HEADS * HD), jnp.bfloat16) for n in (1, 2, 1)]
    return pl.pallas_call(
        grads_kernel,
        out_shape=outs,
        in_specs=[smem()] * 2 + [vmem()] * (len(args) - 2),
        out_specs=[vmem()] * len(outs),
        scratch_shapes=[
            pltpu.VMEM((NY, ROWS), jnp.float32),
            pltpu.VMEM((NY, ROWS), jnp.float32),
            pltpu.VMEM((4 * BLOCK, ROWS), jnp.bfloat16),
            pltpu.VMEM((4 * BLOCK, ROWS), jnp.bfloat16),
            pltpu.VMEM((2 * NZ * BLOCK, HD), jnp.float32),
            pltpu.VMEM((2 * NZ * BLOCK, HD), jnp.float32),
            pltpu.VMEM((NY * HD, ROWS), jnp.float32),
        ],
        compiler_params=pltpu.CompilerParams(vmem_limit_bytes=VMEM_LIMIT),
        cost_estimate=cost(5, 20),
    )(*args)


def swap(array, flip):
    return lax.ppermute(array, "inner", [(i, i ^ flip) for i in range(GROUP)])


def across(array, by):
    outer = lax.axis_size("outer")
    pairs = [
        (o * GROUP + i, (o + by) * GROUP + (i ^ (0 if max(o, o + by) % 2 else FAR)))
        for o in range(outer)
        if 0 <= o + by < outer
        for i in range(GROUP)
    ]
    return lax.ppermute(array, ("outer", "inner"), pairs)


def add_low(*terms):
    total = terms[0].astype(jnp.float32)
    for term in terms[1:]:
        total = total + term.astype(jnp.float32)
    return total.astype(jnp.bfloat16)


def shards(queries, keys, values, grad_out, doc_ids, block_order):
    one = 2 * BLOCK
    ids = jnp.stack([lax.axis_index("outer"), lax.axis_index("inner")]).astype(jnp.int32)
    meta = jnp.concatenate([doc_ids, block_order, ids])
    own = jnp.concatenate([keys, values], axis=0)
    qg0 = jnp.concatenate([queries, grad_out], axis=0)

    own4 = swap(own, 4)
    qg_later, _ = lax.optimization_barrier((qg0, own4))
    qg1 = swap(qg0, NZ)
    qg3 = swap(qg_later, 3 * NZ)
    qg2 = swap(qg_later, 2 * NZ)
    own_pair = jnp.concatenate([own, own4], axis=0)
    before_pair = across(own_pair, 1)
    own_low = jnp.concatenate([own_pair, swap(own_pair, 2)], axis=0)
    own_high = swap(own_low, 1)
    before_low = jnp.concatenate([before_pair, swap(before_pair, 2)], axis=0)
    before_low, qg1, qg3 = lax.optimization_barrier((before_low, qg1, qg3))
    before_high = swap(before_low, 1)

    stats, own_k, own_v, own_lists, qs, gs = run_stats(
        False, meta, own_low, own_high, qg0, qg1, qg2, qg3
    )
    stats, ks, vs, _, every = run_stats(
        True, meta, before_low, before_high, qs, gs, stats, own_k, own_v, own_lists
    )
    along_y = [[y * NZ + z for y in range(NY)] for z in range(NZ)]
    all_stats = lax.all_gather(stats, "inner", axis=0, tiled=True, axis_index_groups=along_y)
    b_high, b_mid, b_pair, o_high, o_mid, o_one, o_zero, dq0, dq12, dq3 = run_grads(
        meta, every, qs, gs, ks, vs, all_stats
    )

    b_near = swap(b_high, 1)
    o_near = swap(o_high, 1)
    e12 = swap(dq12, NZ)
    b_far = swap(add_low(b_mid, b_near[2 * one :]), 2)
    back = across(add_low(b_pair, b_near[: 2 * one], b_far), -1)
    o_far = swap(add_low(o_mid, o_near[2 * one :]), 2)
    e3 = swap(add_low(dq3, e12[BLOCK:]), 3 * NZ)
    o_four = swap(add_low(o_one, o_near[one : 2 * one], o_far[one:], back[one:]), 4)
    grad_queries = add_low(dq0, e12[:BLOCK], e3)
    o_four, grad_queries = lax.optimization_barrier((o_four, grad_queries))
    terms = (o_zero, o_near[:one], o_far[:one], back[:one], o_four)
    grad_keys = add_low(*[term[:BLOCK] for term in terms])
    grad_values = add_low(*[term[BLOCK:] for term in terms])
    return grad_queries, grad_keys, grad_values


def solution(mesh):
    rows = P(("outer", "inner"), None)
    return jax.shard_map(
        shards,
        mesh=mesh,
        in_specs=(rows, rows, rows, rows, P(), P()),
        out_specs=(rows, rows, rows),
        check_vma=False,
    )
```
